32 devices in a mesh: ens: 4 (over y, x), grid: 8 (over z, core).
Axes of the slice: x: 2, y: 2, z: 4, core: 2. Of those that a mesh axis runs over, the one named last changes fastest.
Arguments:
- grid_latent: bfloat16 [4, 8192, 512], P('ens', 'grid'), may hold values from -6 to 6
- mesh_latent: bfloat16 [4, 1024, 512], P('ens', 'grid'), may hold values from -6 to 6
- cotangent: bfloat16 [4, 1024, 512], P('ens', 'grid'), may hold values from -6 to 6
- edge_weights: bfloat16 [64, 2, 128, 128], P('grid'), may hold values from -0.125 to 0.125
- edge_targets: int32 [64, 2], P('grid'), may hold values from 0 to 7, as said below
- mesh_weights: bfloat16 [8, 2, 128, 128], P('grid'), may hold values from -0.375 to 0.375
- mesh_sources: int32 [8, 2], P('grid'), may hold values from 0 to 7, as said below
- encode_weight: bfloat16 [512, 512], replicated, may hold values from -0.25 to 0.25
- aggregate_weight: bfloat16 [512, 512], replicated, may hold values from -0.25 to 0.25
- process_weight: bfloat16 [512, 512], replicated, may hold values from -0.25 to 0.25
Outputs:
- result: bfloat16 [4, 1024, 512], P('ens', 'grid')
- grid_grad: bfloat16 [4, 8192, 512], P('ens', 'grid')
- grad_encode: float32 [512, 512], P('grid')
The draws below stay inside these ranges and needn't reach their ends.
Inputs may be any that keep to these rules, and one draw needn't show every extreme that they name: `edge_targets`: row b names 2 different mesh blocks, each at most one away from b // 8. `mesh_sources`: row t names 2 different mesh blocks, each at most one away from t.
All inputs are finite; a program needn't handle non-finite values.
Results may differ from the reference program's by a relative error of at most 0.018.
Values may be sent and summed in bfloat16 or wider, within the bound.
A program may use at most 64 MiB of HBM per device.

```python
import jax
import jax.numpy as jnp
from jax import lax

D = 512
BLK = 128
K = 2
KM = 2
GB_DEV = 8
MEMBERS = 4
GRID_BLOCKS = 64
GRID = 8192
MESH_BLOCKS = 8
MESH = 1024


def pick_near(key, count, spread, picks):
    owner = jnp.arange(count, dtype=jnp.int32) // spread
    offsets = jnp.arange(3, dtype=jnp.int32)
    scores = jax.random.randint(key, (count, 3), 0, 1000, dtype=jnp.int32) * 3 + offsets
    nearby = owner[:, None] + offsets - 1
    inside = (nearby >= 0) & (nearby < MESH_BLOCKS)
    scores = jnp.where(inside, scores, -1)
    unused, order = lax.top_k(scores, picks)
    return jnp.take_along_axis(nearby, order, 1).astype(jnp.int32)


def draw_edge_targets(key, part):
    key = jax.random.fold_in(key, 11)
    return pick_near(key, GRID_BLOCKS, GB_DEV, K)


def draw_mesh_sources(key, part):
    key = jax.random.fold_in(key, 17)
    return pick_near(key, MESH_BLOCKS, 1, KM)


def block_levels(stream_key, extent, split, low, largest):
    loudness = 1.0
    for dim, blocks in split:
        steps = jax.random.uniform(jax.random.fold_in(jax.random.fold_in(stream_key, 6), dim), (blocks,), jnp.float32, low / len(split), largest / len(split))
        loudness = loudness * jnp.repeat(jnp.exp(steps), extent[dim] // blocks).reshape((-1,) + (1,) * (len(extent) - 1 - dim))
    return loudness


def bell_draw(rng, extent, deviation, bound, cuts=(), kind=jnp.bfloat16):
    values = jax.random.normal(rng, extent, jnp.float32) * deviation
    if len(cuts) > 0:
        values = block_levels(rng, extent, cuts, -0.22, 0.18) * values
    return jnp.clip(values, min=-bound, max=bound).astype(kind)


def setup_inputs(seed: int = 0) -> dict:
    splits = jax.random.split(jax.random.key(seed), 11)
    grid_latent = bell_draw(splits[0], (MEMBERS, GRID, D), 1.0, 6.0, ((0, 4), (1, 8)))
    mesh_latent = bell_draw(splits[1], (MEMBERS, MESH, D), 1.0, 6.0, ((0, 4), (1, 8)))
    cotangent = bell_draw(splits[2], (MEMBERS, MESH, D), 1.0, 6.0, ((0, 4), (1, 8)))
    edge_weights = bell_draw(splits[3], (GRID_BLOCKS, K, BLK, BLK), (GB_DEV * K * BLK) ** -0.5, 0.125, ((0, 8),))
    edge_targets = draw_edge_targets(jax.random.fold_in(splits[10], 71), 0)
    mesh_weights = bell_draw(splits[5], (MESH_BLOCKS, KM, BLK, BLK), (KM * BLK) ** -0.5, 0.375, ((0, 8),))
    mesh_sources = draw_mesh_sources(jax.random.fold_in(splits[10], 71), 0)
    encode_weight = bell_draw(splits[7], (D, D), D ** -0.5, 0.25)
    aggregate_weight = bell_draw(splits[8], (D, D), D ** -0.5, 0.25)
    process_weight = bell_draw(splits[9], (D, D), D ** -0.5, 0.25)
    return dict(grid_latent=grid_latent, mesh_latent=mesh_latent, cotangent=cotangent, edge_weights=edge_weights, edge_targets=edge_targets, mesh_weights=mesh_weights, mesh_sources=mesh_sources, encode_weight=encode_weight, aggregate_weight=aggregate_weight, process_weight=process_weight)


def silu_slope(value):
    sig = jax.nn.sigmoid(value)
    return sig * (1.0 + value * (1.0 - sig))


def spread_blocks(parts):
    zero_block = jnp.zeros_like(parts[:1, 0])
    from_lower = jnp.concatenate([zero_block, parts[:-1, 2]], 0)
    from_upper = jnp.concatenate([parts[1:, 0], zero_block], 0)
    return parts[:, 1] + from_lower + from_upper


def reference(grid_latent, mesh_latent, cotangent, edge_weights, edge_targets, mesh_weights, mesh_sources, encode_weight, aggregate_weight, process_weight):
    owner = jnp.arange(GRID_BLOCKS, dtype=jnp.int32) // GB_DEV
    three = jnp.arange(3, dtype=jnp.int32)
    target_pick = ((edge_targets - owner[:, None] + 1)[:, :, None] == three).astype(jnp.float32)
    ident = jnp.arange(MESH_BLOCKS, dtype=jnp.int32)
    source_pick = ((mesh_sources - ident[:, None] + 1)[:, :, None] == three).astype(jnp.float32)
    edge_float = edge_weights.astype(jnp.float32)
    mesh_float = mesh_weights.astype(jnp.float32)

    def member(packed):
        grid_x, mesh_h, upstream_in = packed
        encoded = jnp.dot(grid_x, encode_weight, preferred_element_type=jnp.float32)
        messages = jax.nn.silu(encoded).astype(jnp.bfloat16).reshape(GRID_BLOCKS, BLK, D)
        products = jnp.einsum('bkac,bcd->bkad', edge_float, messages.astype(jnp.float32))
        panels = jnp.einsum('bkj,bkad->bjad', target_pick, products)
        panels = panels.reshape(MESH_BLOCKS, GB_DEV, 3, BLK, D).sum(1).astype(jnp.bfloat16)
        aggregated = spread_blocks(panels.astype(jnp.float32)).astype(jnp.bfloat16).reshape(MESH, D)
        mesh_pre = jnp.dot(aggregated, aggregate_weight, preferred_element_type=jnp.float32)
        updated = (mesh_h.astype(jnp.float32) + jax.nn.silu(mesh_pre)).astype(jnp.bfloat16)
        zero_block = jnp.zeros((1, BLK, D), jnp.bfloat16)
        padded = jnp.concatenate([zero_block, updated.reshape(MESH_BLOCKS, BLK, D), zero_block], 0)
        chosen = padded[(mesh_sources + 1).astype(jnp.int32)]
        processed = jnp.einsum('tkab,tkbd->tad', mesh_float, chosen.astype(jnp.float32))
        processed = processed.astype(jnp.bfloat16).reshape(MESH, D)
        proc_pre = jnp.dot(processed, process_weight, preferred_element_type=jnp.float32)
        result = (updated.astype(jnp.float32) + jax.nn.silu(proc_pre)).astype(jnp.bfloat16)
        upstream = upstream_in.astype(jnp.float32)
        proc_delta = (upstream * silu_slope(proc_pre)).astype(jnp.bfloat16)
        proc_back = jnp.dot(proc_delta, process_weight.T, preferred_element_type=jnp.float32)
        proc_back = proc_back.astype(jnp.bfloat16).reshape(MESH_BLOCKS, BLK, D)
        back = jnp.einsum('tkab,tad->tkbd', mesh_float, proc_back.astype(jnp.float32))
        pushed = jnp.einsum('tkj,tkbd->tjbd', source_pick, back).astype(jnp.bfloat16)
        mesh_grad = upstream + spread_blocks(pushed.astype(jnp.float32)).reshape(MESH, D)
        mesh_delta = (mesh_grad * silu_slope(mesh_pre)).astype(jnp.bfloat16)
        agg_grad = jnp.dot(mesh_delta, aggregate_weight.T, preferred_element_type=jnp.float32)
        agg_grad = agg_grad.astype(jnp.bfloat16).reshape(MESH_BLOCKS, BLK, D)
        padded_grad = jnp.concatenate([zero_block, agg_grad, zero_block], 0)
        picked = padded_grad[(edge_targets + 1).astype(jnp.int32)]
        message_grad = jnp.einsum('bkac,bkad->bcd', edge_float, picked.astype(jnp.float32)).reshape(GRID, D)
        enc_delta = (message_grad * silu_slope(encoded)).astype(jnp.bfloat16)
        grad_enc = jnp.dot(grid_x.T, enc_delta, preferred_element_type=jnp.float32)
        grid_grad = jnp.dot(enc_delta, encode_weight.T, preferred_element_type=jnp.float32).astype(jnp.bfloat16)
        return result, grid_grad, grad_enc

    result, grid_grad, grad_enc = lax.map(member, (grid_latent, mesh_latent, cotangent))
    grid_scale = 1.0 / (float(MEMBERS * GRID) ** 0.5)
    grad_encode = jnp.sum(grad_enc, 0) * grid_scale
    return (result, grid_grad, grad_encode)
```

```python
import functools

import jax
import jax.numpy as jnp
from jax import lax
from jax.experimental import pallas as pl
from jax.experimental.pallas import tpu as pltpu
from jax.sharding import PartitionSpec as P

MESH = pl.DeviceIdType.MESH
F32 = jnp.float32
BF16 = jnp.bfloat16
CHUNKS = 4


def sigmoid(value):
    return 0.5 + 0.5 * jnp.tanh(0.5 * value)


def slope_of(value):
    sig = sigmoid(value)
    return sig * (1.0 + value * (1.0 - sig))


def dot(a, b):
    return jnp.dot(a, b, preferred_element_type=F32)


def dot_t(a, b):
    return lax.dot_general(a, b, (((1,), (1,)), ((), ())), preferred_element_type=F32)


def kernel(
    bands, members, scale, fused,
    x_h, mesh_h, cot_h, edge_h, targets, mweight_h, sources, enc_w_h, agg_w_h, proc_w_h,
    result_h, grid_h, final_h,
    x, mesh, cot, edge, mweight, enc_w, agg_w, proc_w,
    wide, wide_own_t, wide_side_t, near, near_t, x_t,
    encoded, messages, panel_out, panel_in, upd, upd_in, push_out, push_in, agg, agg_in,
    own_grad, enc_delta, grid_out, result,
    part, part_out, pair_in, quarter, quarter_out, ens_in, summed, summed_out, z_in, final,
    in_sem, out_sem, halo_send, halo_recv, a_send, a_recv, b_send, b_recv, c_send, c_recv, d_send, d_recv,
):
    me = lax.axis_index("grid")
    ens = lax.axis_index("ens")
    core = lax.rem(me, 2)
    level = me // 2
    levels = bands // 2
    rows = mesh.shape[0]
    total = x.shape[0]
    blocks = total // rows
    step = total // CHUNKS
    width = x.shape[1]
    far = 2 * core - 1
    far_there = (me + far >= 0) & (me + far < bands)

    def both(act):
        pl.when(far_there)(lambda: act(far))
        act(-far)

    def local(src, dst, sem):
        copy = pltpu.make_async_copy(src, dst, sem)
        copy.start()
        return copy

    edge_copy = local(edge_h, edge, in_sem.at[0])
    enc_copy = local(enc_w_h, enc_w, in_sem.at[1])
    x_copies = [
        local(x_h.at[0, pl.ds(i * step, step)], x.at[pl.ds(i * step, step)], in_sem.at[8 + i])
        for i in range(CHUNKS)
    ]
    agg_copy = local(agg_w_h, agg_w, in_sem.at[2])
    mesh_copy = local(mesh_h.at[0], mesh, in_sem.at[3])
    mweight_copy = local(mweight_h.at[0], mweight, in_sem.at[4])
    proc_copy = local(proc_w_h, proc_w, in_sem.at[5])
    cot_copy = local(cot_h.at[0], cot, in_sem.at[6])

    barrier = pltpu.get_barrier_semaphore()

    def greet(**where):
        pl.semaphore_signal(barrier, inc=1, device_id=where, device_id_type=MESH)

    both(lambda off: greet(grid=me + off))
    expected = 1 + far_there.astype(jnp.int32)
    if fused:
        for d in range(1, members):
            greet(ens=lax.rem(ens + d, members))
        for d in range(1, levels):
            greet(grid=lax.rem(level + d, levels) * 2 + core)
        expected = expected + (members - 1) + (levels - 1)

    @pl.when(jnp.logical_not(far_there))
    def clear():
        slot = (1 + far) // 2
        for ref in (panel_in, upd_in, push_in, agg_in):
            ref[slot] = jnp.zeros(ref.shape[1:], ref.dtype)

    edge_copy.wait()
    for b in range(blocks):
        first = edge[b, 0].astype(F32)
        second = edge[b, 1].astype(F32)
        for j in range(3):
            hit = [jnp.where(targets[b, k] - me + 1 == j, 1.0, 0.0).astype(F32) for k in range(2)]
            wide[j, :, b * rows:(b + 1) * rows] = (first * hit[0] + second * hit[1]).astype(BF16)

    enc_copy.wait()
    for i in range(CHUNKS):
        x_copies[i].wait()
        span = pl.ds(i * step, step)
        value = dot(x[span], enc_w[...])
        encoded[span] = value
        messages[span] = (value * sigmoid(value)).astype(BF16)

    def halo(turn, source, landing, off):
        slot = (1 - off) // 2
        return pltpu.make_async_remote_copy(
            src_ref=source,
            dst_ref=landing.at[slot],
            send_sem=halo_send.at[turn, slot],
            recv_sem=halo_recv.at[turn, slot],
            device_id={"grid": me + off},
            device_id_type=MESH,
        )

    def received(turn, landing):
        act = lambda off: halo(turn, landing.at[(1 - off) // 2], landing, off).wait_recv()
        act(far)
        pl.when(far_there)(lambda: act(-far))

    def sent(turn, landing):
        both(lambda off: halo(turn, landing.at[(1 - off) // 2], landing, off).wait_send())

    pl.semaphore_wait(barrier, expected)
    for off, there in ((far, far_there), (-far, None)):
        panel_out[(1 - off) // 2] = dot(wide[1 + off], messages[...]).astype(BF16)
        go = functools.partial(halo, 0, panel_out.at[(1 - off) // 2], panel_in, off)
        if there is None:
            go().start()
        else:
            pl.when(there)(lambda: go().start())

    own_panel = dot(wide[1], messages[...])
    for i in range(CHUNKS):
        span = pl.ds(i * step, step)
        encoded[span] = slope_of(encoded[span])
    for b in range(blocks):
        span = pl.ds(b * rows, rows)
        wide_own_t[span] = wide[1, :, b * rows:(b + 1) * rows].T
        wide_side_t[span, 0:rows] = wide[0, :, b * rows:(b + 1) * rows].T
        wide_side_t[span, rows:2 * rows] = wide[2, :, b * rows:(b + 1) * rows].T
    mweight_copy.wait()
    first = mweight[0].astype(F32)
    second = mweight[1].astype(F32)
    for j in range(3):
        hit = [jnp.where(sources[0, k] - me + 1 == j, 1.0, 0.0).astype(F32) for k in range(2)]
        mixed = (first * hit[0] + second * hit[1]).astype(BF16)
        near[j] = mixed
        near_t[j] = mixed.T
    mesh_copy.wait()
    agg_copy.wait()

    received(0, panel_in)
    aggregated = own_panel + panel_in[0].astype(F32) + panel_in[1].astype(F32)
    mesh_pre = dot(aggregated.astype(BF16), agg_w[...])
    mesh_sig = sigmoid(mesh_pre)
    updated = (mesh[...].astype(F32) + mesh_pre * mesh_sig).astype(BF16)
    upd[...] = updated
    both(lambda off: halo(1, upd, upd_in, off).start())

    processed = dot(near[1], updated)
    mesh_slope = mesh_sig * (1.0 + mesh_pre * (1.0 - mesh_sig))
    deep = width // CHUNKS
    for i in range(CHUNKS):
        x_t[i] = x[:, i * deep:(i + 1) * deep].T
    proc_copy.wait()
    cot_copy.wait()
    upstream = cot[...].astype(F32)

    received(1, upd_in)
    processed = processed + dot(near[0], upd_in[0]) + dot(near[2], upd_in[1])
    proc_pre = dot(processed.astype(BF16), proc_w[...])
    proc_sig = sigmoid(proc_pre)
    proc_slope = proc_sig * (1.0 + proc_pre * (1.0 - proc_sig))
    proc_back = dot_t((upstream * proc_slope).astype(BF16), proc_w[...]).astype(BF16)
    for off, there in ((far, far_there), (-far, None)):
        push_out[(1 - off) // 2] = dot(near_t[1 + off], proc_back).astype(BF16)
        go = functools.partial(halo, 2, push_out.at[(1 - off) // 2], push_in, off)
        if there is None:
            go().start()
        else:
            pl.when(there)(lambda: go().start())
    mesh_grad = upstream + dot(near_t[1], proc_back)
    result[...] = (upd[...].astype(F32) + proc_pre * proc_sig).astype(BF16)
    result_copy = local(result, result_h.at[0], out_sem.at[CHUNKS])

    received(2, push_in)
    mesh_grad = mesh_grad + push_in[0].astype(F32) + push_in[1].astype(F32)
    agg_grad = dot_t((mesh_grad * mesh_slope).astype(BF16), agg_w[...]).astype(BF16)
    agg[...] = agg_grad
    both(lambda off: halo(3, agg, agg_in, off).start())
    for i in range(CHUNKS):
        span = pl.ds(i * step, step)
        own_grad[span] = dot(wide_own_t[span], agg_grad)

    received(3, agg_in)
    sides = agg_in[...].reshape(2 * rows, width)
    for i in range(CHUNKS):
        span = pl.ds(i * step, step)
        grad = own_grad[span] + dot(wide_side_t[span], sides)
        enc_delta[span] = (grad * encoded[span]).astype(BF16)

    def grid_part(i):
        span = pl.ds(i * step, step)
        grid_out[span] = dot_t(enc_delta[span], enc_w[...]).astype(BF16)
        return local(grid_out.at[span], grid_h.at[0, span], out_sem.at[i])

    if not fused:
        for i in range(CHUNKS):
            part[i] = dot(x_t[i], enc_delta[...]) * scale
        final_copy = local(part, final_h, out_sem.at[CHUNKS + 1])
        grid_copies = [grid_part(i) for i in range(CHUNKS)]
    else:
        share = part.shape[2]
        mine = share // members

        def pair(z):
            return pltpu.make_async_remote_copy(
                src_ref=part_out.at[z, 1 - core], dst_ref=pair_in.at[z],
                send_sem=a_send.at[z], recv_sem=a_recv.at[z],
                device_id={"grid": me + 1 - 2 * core}, device_id_type=MESH)

        def across(z, d, arriving):
            peer = lax.rem(ens + d, members)
            slot = peer if arriving else ens
            return pltpu.make_async_remote_copy(
                src_ref=quarter_out.at[z, peer], dst_ref=ens_in.at[z, slot],
                send_sem=b_send.at[z, peer], recv_sem=b_recv.at[z, slot],
                device_id={"ens": peer}, device_id_type=MESH)

        def along(d, arriving):
            peer = lax.rem(level + d, levels)
            slot = peer if arriving else level
            return pltpu.make_async_remote_copy(
                src_ref=summed_out.at[peer], dst_ref=z_in.at[slot],
                send_sem=c_send.at[peer], recv_sem=c_recv.at[slot],
                device_id={"grid": peer * 2 + core}, device_id_type=MESH)

        def gather(d, arriving):
            peer = lax.rem(ens + d, members)
            slot = peer if arriving else ens
            return pltpu.make_async_remote_copy(
                src_ref=final.at[ens], dst_ref=final.at[slot],
                send_sem=d_send.at[peer], recv_sem=d_recv.at[slot],
                device_id={"ens": peer}, device_id_type=MESH)

        order = [lax.rem(level + d, levels) for d in list(range(1, levels)) + [0]]
        for z in order:
            value = (dot(x_t[z], enc_delta[...]) * scale).reshape(2, share, width)
            part[z] = value
            part_out[z] = value.astype(BF16)
            pair(z).start()
        grid_copies = [grid_part(0)]
        for z in order:
            pair(z).wait_recv()
            value = part[z, core] + pair_in[z].astype(F32)
            value = value.reshape(members, mine, width)
            quarter[z] = value
            quarter_out[z] = value.astype(BF16)
            for d in range(1, members):
                across(z, d, False).start()
        grid_copies += [grid_part(i) for i in range(1, CHUNKS)]
        for n, z in enumerate(order):
            value = quarter[z, ens]
            for d in range(1, members):
                across(z, d, True).wait_recv()
                value = value + ens_in[z, lax.rem(ens + d, members)].astype(F32)
            if n < levels - 1:
                summed_out[z] = value.astype(BF16)
                along(n + 1, False).start()
            else:
                summed[...] = value
        value = summed[...]
        for d in range(1, levels):
            along(d, True).wait_recv()
            value = value + z_in[lax.rem(level + d, levels)].astype(F32)
        final[ens] = value
        for d in range(1, members):
            gather(d, False).start()
        for d in range(1, members):
            gather(d, True).wait_recv()
        final_copy = local(final, final_h, out_sem.at[CHUNKS + 1])
        for z in order:
            pair(z).wait_send()
            for d in range(1, members):
                across(z, d, False).wait_send()
        for d in range(1, levels):
            along(d, False).wait_send()
        for d in range(1, members):
            gather(d, False).wait_send()

    for turn, landing in enumerate((panel_in, upd_in, push_in, agg_in)):
        sent(turn, landing)
    result_copy.wait()
    for copy in grid_copies:
        copy.wait()
    final_copy.wait()


def on_device(
    bands, members,
    grid_latent, mesh_latent, cotangent, edge_weights, edge_targets, mesh_weights, mesh_sources,
    encode_weight, aggregate_weight, process_weight,
):
    unused, total, width = grid_latent.shape
    rows = mesh_latent.shape[1]
    share = width // bands
    levels = max(bands // 2, 1)
    fused = bands % 2 == 0 and levels == CHUNKS and share % (16 * members) == 0
    scale = 1.0 / float(members * total * bands) ** 0.5
    mine = share // members if fused else 16
    gshape = (CHUNKS, 2, width // CHUNKS // 2, width) if fused else (CHUNKS, width // CHUNKS, width)
    last = (members, mine, width) if fused else gshape
    vm = pltpu.VMEM
    dma = pltpu.SemaphoreType.DMA
    panel = (2, rows, width)
    quarters = (CHUNKS, members, mine, width)
    scratch = [
        vm((total, width), BF16), vm((rows, width), BF16), vm((rows, width), BF16),
        vm(edge_weights.shape, BF16), vm(mesh_weights.shape[1:], BF16),
        vm((width, width), BF16), vm((width, width), BF16), vm((width, width), BF16),
        vm((3, rows, total), BF16), vm((total, rows), BF16), vm((total, 2 * rows), BF16),
        vm((3, rows, rows), BF16), vm((3, rows, rows), BF16), vm((CHUNKS, width // CHUNKS, total), BF16),
        vm((total, width), F32), vm((total, width), BF16),
        vm(panel, BF16), vm(panel, BF16), vm((rows, width), BF16), vm(panel, BF16),
        vm(panel, BF16), vm(panel, BF16), vm((rows, width), BF16), vm(panel, BF16),
        vm((total, width), F32), vm((total, width), BF16), vm((total, width), BF16), vm((rows, width), BF16),
        vm(gshape, F32), vm(gshape, BF16), vm((CHUNKS, width // CHUNKS // 2, width), BF16),
        vm(quarters, F32), vm(quarters, BF16), vm(quarters, BF16),
        vm((mine, width), F32), vm((CHUNKS, mine, width), BF16), vm((CHUNKS, mine, width), BF16),
        vm((members, mine, width), F32),
        dma((8 + CHUNKS,)), dma((CHUNKS + 2,)), dma((4, 2)), dma((4, 2)),
        dma((CHUNKS,)), dma((CHUNKS,)), dma((CHUNKS, members)), dma((CHUNKS, members)),
        dma((CHUNKS,)), dma((CHUNKS,)), dma((members,)), dma((members,)),
    ]
    hbm = pl.BlockSpec(memory_space=pl.ANY)
    smem = pl.BlockSpec(memory_space=pltpu.SMEM)
    result, grid_grad, grad = pl.pallas_call(
        functools.partial(kernel, bands, members, scale, fused),
        out_shape=(
            jax.ShapeDtypeStruct(mesh_latent.shape, BF16),
            jax.ShapeDtypeStruct(grid_latent.shape, BF16),
            jax.ShapeDtypeStruct(last, F32),
        ),
        in_specs=[hbm, hbm, hbm, hbm, smem, hbm, smem, hbm, hbm, hbm],
        out_specs=(hbm, hbm, hbm),
        scratch_shapes=scratch,
        compiler_params=pltpu.CompilerParams(
            collective_id=0, has_side_effects=True, vmem_limit_bytes=40 * 1024 * 1024
        ),
    )(
        grid_latent, mesh_latent, cotangent, edge_weights, edge_targets, mesh_weights, mesh_sources,
        encode_weight, aggregate_weight, process_weight,
    )
    if fused:
        grad = grad.reshape(share, width)
    else:
        summed = lax.psum(grad.reshape(width, width), ("ens", "grid"))
        grad = lax.dynamic_slice_in_dim(summed, lax.axis_index("grid") * share, share, 0)
    return result, grid_grad, grad


def solution(mesh):
    return jax.shard_map(
        functools.partial(on_device, mesh.shape["grid"], mesh.shape["ens"]),
        mesh=mesh,
        in_specs=(
            P("ens", "grid", None),
            P("ens", "grid", None),
            P("ens", "grid", None),
            P("grid", None, None, None),
            P("grid", None),
            P("grid", None, None, None),
            P("grid", None),
            P(),
            P(),
            P(),
        ),
        out_specs=(P("ens", "grid", None), P("ens", "grid", None), P("grid", None)),
        check_vma=False,
    )
```

```python
import functools

import jax
import jax.numpy as jnp
from jax import lax
from jax.experimental import pallas as pl
from jax.experimental.pallas import tpu as pltpu
from jax.sharding import PartitionSpec as P

MESH = pl.DeviceIdType.MESH
F32 = jnp.float32
BF16 = jnp.bfloat16
CHUNKS = 4


def sigmoid(value):
    return 0.5 + 0.5 * jnp.tanh(0.5 * value)


def slope_of(value):
    sig = sigmoid(value)
    return sig * (1.0 + value * (1.0 - sig))


def dot(a, b):
    return jnp.dot(a, b, preferred_element_type=F32)


def dot_t(a, b):
    return lax.dot_general(a, b, (((1,), (1,)), ((), ())), preferred_element_type=F32)


def kernel(
    bands, members, scale, fused,
    x_h, mesh_h, cot_h, edge_h, targets_h, mweight_h, sources_h, enc_w_h, agg_w_h, proc_w_h,
    result_h, grid_h, final_h,
    x, mesh, cot, edge, targets, mweight, sources, enc_w, agg_w, proc_w,
    wide, wide_own_t, wide_side_t, near, near_t, x_t,
    encoded, messages, panel_out, panel_in, upd, upd_in, push_out, push_in, agg, agg_in,
    own_grad, enc_delta, grid_out, result,
    part, part_out, pair_in, quarter, quarter_out, ens_in, summed, summed_out, z_in, final, final_out,
    in_sem, out_sem, halo_send, halo_recv, a_send, a_recv, b_send, b_recv, c_send, c_recv, d_send, d_recv,
):
    me = lax.axis_index("grid")
    ens = lax.axis_index("ens")
    core = lax.rem(me, 2)
    level = me // 2
    levels = bands // 2
    rows = mesh.shape[0]
    total = x.shape[0]
    blocks = total // rows
    step = total // CHUNKS
    width = x.shape[1]
    far = 2 * core - 1
    far_there = (me + far >= 0) & (me + far < bands)

    def both(act):
        pl.when(far_there)(lambda: act(far))
        act(-far)

    def local(src, dst, sem):
        copy = pltpu.make_async_copy(src, dst, sem)
        copy.start()
        return copy

    targets_copy = local(targets_h, targets, in_sem.at[7])
    edge_copy = local(edge_h, edge, in_sem.at[0])
    enc_copy = local(enc_w_h, enc_w, in_sem.at[1])
    x_copies = [
        local(x_h.at[0, pl.ds(i * step, step)], x.at[pl.ds(i * step, step)], in_sem.at[8 + i])
        for i in range(CHUNKS)
    ]
    agg_copy = local(agg_w_h, agg_w, in_sem.at[2])
    mesh_copy = local(mesh_h.at[0], mesh, in_sem.at[3])
    mweight_copy = local(mweight_h.at[0], mweight, in_sem.at[4])
    proc_copy = local(proc_w_h, proc_w, in_sem.at[5])
    cot_copy = local(cot_h.at[0], cot, in_sem.at[6])
    sources_copy = local(sources_h, sources, in_sem.at[8 + CHUNKS])

    barrier = pltpu.get_barrier_semaphore()

    def greet(**where):
        pl.semaphore_signal(barrier, inc=1, device_id=where, device_id_type=MESH)

    both(lambda off: greet(grid=me + off))
    expected = 1 + far_there.astype(jnp.int32)
    if fused:
        for d in range(1, members):
            greet(ens=lax.rem(ens + d, members))
        for d in range(1, levels):
            greet(grid=lax.rem(level + d, levels) * 2 + core)
        expected = expected + (members - 1) + (levels - 1)

    @pl.when(jnp.logical_not(far_there))
    def clear():
        slot = (1 + far) // 2
        for ref in (panel_in, upd_in, push_in, agg_in):
            ref[slot] = jnp.zeros(ref.shape[1:], ref.dtype)

    targets_copy.wait()
    edge_copy.wait()
    for b in range(blocks):
        first = edge[b, 0].astype(F32)
        second = edge[b, 1].astype(F32)
        for j in range(3):
            hit = [jnp.where(targets[k, b] - me + 1 == j, 1.0, 0.0).astype(F32) for k in range(2)]
            wide[j, :, b * rows:(b + 1) * rows] = (first * hit[0] + second * hit[1]).astype(BF16)

    enc_copy.wait()
    for i in range(CHUNKS):
        x_copies[i].wait()
        span = pl.ds(i * step, step)
        value = dot(x[span], enc_w[...])
        encoded[span] = value
        messages[span] = (value * sigmoid(value)).astype(BF16)

    def halo(turn, source, landing, off):
        slot = (1 - off) // 2
        return pltpu.make_async_remote_copy(
            src_ref=source,
            dst_ref=landing.at[slot],
            send_sem=halo_send.at[turn, slot],
            recv_sem=halo_recv.at[turn, slot],
            device_id={"grid": me + off},
            device_id_type=MESH,
        )

    def received(turn, landing):
        act = lambda off: halo(turn, landing.at[(1 - off) // 2], landing, off).wait_recv()
        act(far)
        pl.when(far_there)(lambda: act(-far))

    def sent(turn, landing):
        both(lambda off: halo(turn, landing.at[(1 - off) // 2], landing, off).wait_send())

    pl.semaphore_wait(barrier, expected)
    for off, there in ((far, far_there), (-far, None)):
        panel_out[(1 - off) // 2] = dot(wide[1 + off], messages[...]).astype(BF16)
        go = functools.partial(halo, 0, panel_out.at[(1 - off) // 2], panel_in, off)
        if there is None:
            go().start()
        else:
            pl.when(there)(lambda: go().start())

    own_panel = dot(wide[1], messages[...])
    for i in range(CHUNKS):
        span = pl.ds(i * step, step)
        encoded[span] = slope_of(encoded[span])
    sources_copy.wait()
    mweight_copy.wait()
    first = mweight[0].astype(F32)
    second = mweight[1].astype(F32)
    for j in range(3):
        hit = [jnp.where(sources[0, k] - me + 1 == j, 1.0, 0.0).astype(F32) for k in range(2)]
        mixed = (first * hit[0] + second * hit[1]).astype(BF16)
        near[j] = mixed
        near_t[j] = mixed.T
    mesh_copy.wait()
    agg_copy.wait()

    received(0, panel_in)
    aggregated = own_panel + panel_in[0].astype(F32) + panel_in[1].astype(F32)
    mesh_pre = dot(aggregated.astype(BF16), agg_w[...])
    mesh_sig = sigmoid(mesh_pre)
    updated = (mesh[...].astype(F32) + mesh_pre * mesh_sig).astype(BF16)
    upd[...] = updated
    both(lambda off: halo(1, upd, upd_in, off).start())

    processed = dot(near[1], updated)
    mesh_slope = mesh_sig * (1.0 + mesh_pre * (1.0 - mesh_sig))
    deep = width // CHUNKS
    for b in range(blocks):
        span = pl.ds(b * rows, rows)
        wide_own_t[span] = wide[1, :, b * rows:(b + 1) * rows].T
        wide_side_t[span, 0:rows] = wide[0, :, b * rows:(b + 1) * rows].T
        wide_side_t[span, rows:2 * rows] = wide[2, :, b * rows:(b + 1) * rows].T
    x_t[0] = x[:, 0:deep].T
    proc_copy.wait()
    cot_copy.wait()
    upstream = cot[...].astype(F32)

    received(1, upd_in)
    processed = processed + dot(near[0], upd_in[0]) + dot(near[2], upd_in[1])
    proc_pre = dot(processed.astype(BF16), proc_w[...])
    proc_sig = sigmoid(proc_pre)
    proc_slope = proc_sig * (1.0 + proc_pre * (1.0 - proc_sig))
    proc_back = dot_t((upstream * proc_slope).astype(BF16), proc_w[...]).astype(BF16)
    for off, there in ((far, far_there), (-far, None)):
        push_out[(1 - off) // 2] = dot(near_t[1 + off], proc_back).astype(BF16)
        go = functools.partial(halo, 2, push_out.at[(1 - off) // 2], push_in, off)
        if there is None:
            go().start()
        else:
            pl.when(there)(lambda: go().start())
    mesh_grad = upstream + dot(near_t[1], proc_back)
    result[...] = (upd[...].astype(F32) + proc_pre * proc_sig).astype(BF16)
    result_copy = local(result, result_h.at[0], out_sem.at[CHUNKS])

    x_t[1] = x[:, deep:2 * deep].T
    x_t[2] = x[:, 2 * deep:3 * deep].T

    received(2, push_in)
    mesh_grad = mesh_grad + push_in[0].astype(F32) + push_in[1].astype(F32)
    agg_grad = dot_t((mesh_grad * mesh_slope).astype(BF16), agg_w[...]).astype(BF16)
    agg[...] = agg_grad
    both(lambda off: halo(3, agg, agg_in, off).start())
    for i in range(CHUNKS):
        span = pl.ds(i * step, step)
        own_grad[span] = dot(wide_own_t[span], agg_grad)

    x_t[3] = x[:, 3 * deep:4 * deep].T

    received(3, agg_in)
    sides = agg_in[...].reshape(2 * rows, width)
    for i in range(CHUNKS):
        span = pl.ds(i * step, step)
        grad = own_grad[span] + dot(wide_side_t[span], sides)
        enc_delta[span] = (grad * encoded[span]).astype(BF16)

    def grid_part(i):
        span = pl.ds(i * step, step)
        grid_out[span] = dot_t(enc_delta[span], enc_w[...]).astype(BF16)
        return local(grid_out.at[span], grid_h.at[0, span], out_sem.at[i])

    if not fused:
        for i in range(CHUNKS):
            part[i] = dot(x_t[i], enc_delta[...]) * scale
        final_copy = local(part, final_h, out_sem.at[CHUNKS + 1])
        grid_copies = [grid_part(i) for i in range(CHUNKS)]
    else:
        share = part.shape[2]
        mine = share // members

        def pair(z):
            return pltpu.make_async_remote_copy(
                src_ref=part_out.at[z, 1 - core], dst_ref=pair_in.at[z],
                send_sem=a_send.at[z], recv_sem=a_recv.at[z],
                device_id={"grid": me + 1 - 2 * core}, device_id_type=MESH)

        def across(z, d, arriving):
            peer = lax.rem(ens + d, members)
            slot = peer if arriving else ens
            return pltpu.make_async_remote_copy(
                src_ref=quarter_out.at[z, peer], dst_ref=ens_in.at[z, slot],
                send_sem=b_send.at[z, peer], recv_sem=b_recv.at[z, slot],
                device_id={"ens": peer}, device_id_type=MESH)

        def along(d, arriving):
            peer = lax.rem(level + d, levels)
            slot = peer if arriving else level
            return pltpu.make_async_remote_copy(
                src_ref=summed_out.at[peer], dst_ref=z_in.at[slot],
                send_sem=c_send.at[peer], recv_sem=c_recv.at[slot],
                device_id={"grid": peer * 2 + core}, device_id_type=MESH)

        def gather(d, arriving):
            peer = lax.rem(ens + d, members)
            slot = peer if arriving else ens
            return pltpu.make_async_remote_copy(
                src_ref=final.at[ens], dst_ref=final.at[slot],
                send_sem=d_send.at[peer], recv_sem=d_recv.at[slot],
                device_id={"ens": peer}, device_id_type=MESH)

        order = [lax.rem(level + d, levels) for d in list(range(1, levels)) + [0]]
        for z in order:
            value = (dot(x_t[z], enc_delta[...]) * scale).reshape(2, share, width)
            part[z] = value
            part_out[z] = value.astype(BF16)
            pair(z).start()
        grid_copies = [grid_part(0)]
        for z in order:
            pair(z).wait_recv()
            value = part[z, core] + pair_in[z].astype(F32)
            value = value.reshape(members, mine, width)
            quarter[z] = value
            quarter_out[z] = value.astype(BF16)
            for d in range(1, members):
                across(z, d, False).start()
        grid_copies += [grid_part(i) for i in range(1, CHUNKS)]
        for n, z in enumerate(order):
            value = quarter[z, ens]
            for d in range(1, members):
                across(z, d, True).wait_recv()
                value = value + ens_in[z, lax.rem(ens + d, members)].astype(F32)
            if n < levels - 1:
                summed_out[z] = value.astype(BF16)
                along(n + 1, False).start()
            else:
                summed[...] = value
        value = summed[...]
        for d in range(1, levels):
            along(d, True).wait_recv()
            value = value + z_in[lax.rem(level + d, levels)].astype(F32)
        final[ens] = value.astype(BF16)
        for d in range(1, members):
            gather(d, False).start()
        for d in range(1, members):
            gather(d, True).wait_recv()
        final_out[...] = final[...].astype(F32)
        final_copy = local(final_out, final_h, out_sem.at[CHUNKS + 1])
        for z in order:
            pair(z).wait_send()
            for d in range(1, members):
                across(z, d, False).wait_send()
        for d in range(1, levels):
            along(d, False).wait_send()
        for d in range(1, members):
            gather(d, False).wait_send()

    for turn, landing in enumerate((panel_in, upd_in, push_in, agg_in)):
        sent(turn, landing)
    result_copy.wait()
    for copy in grid_copies:
        copy.wait()
    final_copy.wait()


def leave(result, grid_grad, grad, result_out, grid_out, grad_out, sem):
    pairs = ((grid_grad, grid_out), (result, result_out), (grad, grad_out))
    copies = [pltpu.make_async_copy(src, dst, sem.at[i]) for i, (src, dst) in enumerate(pairs)]
    for copy in copies:
        copy.start()
    for copy in copies:
        copy.wait()


def on_device(
    bands, members,
    grid_latent, mesh_latent, cotangent, edge_weights, edge_targets, mesh_weights, mesh_sources,
    encode_weight, aggregate_weight, process_weight,
):
    unused, total, width = grid_latent.shape
    rows = mesh_latent.shape[1]
    share = width // bands
    levels = max(bands // 2, 1)
    fused = bands % 2 == 0 and levels == CHUNKS and share % (16 * members) == 0
    scale = 1.0 / float(members * total * bands) ** 0.5
    mine = share // members if fused else 16
    gshape = (CHUNKS, 2, width // CHUNKS // 2, width) if fused else (CHUNKS, width // CHUNKS, width)
    last = (members, mine, width) if fused else gshape
    vm = pltpu.VMEM
    dma = pltpu.SemaphoreType.DMA
    panel = (2, rows, width)
    quarters = (CHUNKS, members, mine, width)
    scratch = [
        vm((total, width), BF16), vm((rows, width), BF16), vm((rows, width), BF16),
        vm(edge_weights.shape, BF16),
        pltpu.SMEM(edge_targets.shape[::-1], jnp.int32), vm(mesh_weights.shape[1:], BF16),
        pltpu.SMEM(mesh_sources.shape, jnp.int32),
        vm((width, width), BF16), vm((width, width), BF16), vm((width, width), BF16),
        vm((3, rows, total), BF16), vm((total, rows), BF16), vm((total, 2 * rows), BF16),
        vm((3, rows, rows), BF16), vm((3, rows, rows), BF16), vm((CHUNKS, width // CHUNKS, total), BF16),
        vm((total, width), F32), vm((total, width), BF16),
        vm(panel, BF16), vm(panel, BF16), vm((rows, width), BF16), vm(panel, BF16),
        vm(panel, BF16), vm(panel, BF16), vm((rows, width), BF16), vm(panel, BF16),
        vm((total, width), F32), vm((total, width), BF16), vm((total, width), BF16), vm((rows, width), BF16),
        vm(gshape, F32), vm(gshape, BF16), vm((CHUNKS, width // CHUNKS // 2, width), BF16),
        vm(quarters, F32), vm(quarters, BF16), vm(quarters, BF16),
        vm((mine, width), F32), vm((CHUNKS, mine, width), BF16), vm((CHUNKS, mine, width), BF16),
        vm((members, mine, width), BF16), vm((members, mine, width), F32),
        dma((9 + CHUNKS,)), dma((CHUNKS + 2,)), dma((4, 2)), dma((4, 2)),
        dma((CHUNKS,)), dma((CHUNKS,)), dma((CHUNKS, members)), dma((CHUNKS, members)),
        dma((CHUNKS,)), dma((CHUNKS,)), dma((members,)), dma((members,)),
    ]
    hbm = pl.BlockSpec(memory_space=pltpu.HBM)
    anywhere = pl.BlockSpec(memory_space=pl.ANY)
    result, grid_grad, grad = pl.pallas_call(
        functools.partial(kernel, bands, members, scale, fused),
        out_shape=(
            jax.ShapeDtypeStruct(mesh_latent.shape, BF16),
            jax.ShapeDtypeStruct(grid_latent.shape, BF16),
            jax.ShapeDtypeStruct(last, F32),
        ),
        in_specs=[hbm] * 10,
        out_specs=(anywhere,) * 3,
        scratch_shapes=scratch,
        compiler_params=pltpu.CompilerParams(
            collective_id=0, has_side_effects=True, vmem_limit_bytes=63 * 1024 * 1024
        ),
    )(
        grid_latent, mesh_latent, cotangent, edge_weights, edge_targets.T, mesh_weights, mesh_sources,
        encode_weight, aggregate_weight, process_weight,
    )
    if fused:
        result, grid_grad, grad = pl.pallas_call(
            leave,
            out_shape=tuple(jax.ShapeDtypeStruct(a.shape, a.dtype) for a in (result, grid_grad, grad)),
            in_specs=[anywhere] * 3,
            out_specs=(hbm,) * 3,
            scratch_shapes=[dma((3,))],
            compiler_params=pltpu.CompilerParams(vmem_limit_bytes=63 * 1024 * 1024),
        )(result, grid_grad, grad)
        grad = grad.reshape(share, width)
    else:
        summed = lax.psum(grad.reshape(width, width), ("ens", "grid"))
        grad = lax.dynamic_slice_in_dim(summed, lax.axis_index("grid") * share, share, 0)
    return result, grid_grad, grad


def solution(mesh):
    return jax.shard_map(
        functools.partial(on_device, mesh.shape["grid"], mesh.shape["ens"]),
        mesh=mesh,
        in_specs=(
            P("ens", "grid", None),
            P("ens", "grid", None),
            P("ens", "grid", None),
            P("grid", None, None, None),
            P("grid", None),
            P("grid", None, None, None),
            P("grid", None),
            P(),
            P(),
            P(),
        ),
        out_specs=(P("ens", "grid", None), P("ens", "grid", None), P("grid", None)),
        check_vma=False,
    )
```

```python
import functools

import jax
import jax.numpy as jnp
from jax import lax
from jax.experimental import pallas as pl
from jax.experimental.pallas import tpu as pltpu
from jax.sharding import PartitionSpec as P

MESH = pl.DeviceIdType.MESH
F32 = jnp.float32
BF16 = jnp.bfloat16
CHUNKS = 4
HALVES = 2


def sigmoid(value):
    return 0.5 + 0.5 * jnp.tanh(0.5 * value)


def slope_of(value):
    sig = sigmoid(value)
    return sig * (1.0 + value * (1.0 - sig))


def dot(a, b):
    return jnp.dot(a, b, preferred_element_type=F32)


def dot_t(a, b):
    return lax.dot_general(a, b, (((1,), (1,)), ((), ())), preferred_element_type=F32)


def kernel(
    bands, members, scale, fused,
    x_h, mesh_h, cot_h, edge_h, targets_h, mweight_h, sources_h, enc_w_h, agg_w_h, proc_w_h,
    result_h, grid_h, final_h,
    x, mesh, cot, edge, targets, mweight, sources, enc_w, agg_w, proc_w,
    wide, wide_own_t, wide_side_t, near, near_t, x_t,
    encoded, panels, panel_out, panel_in, upd, upd_in, push_out, push_in, agg, agg_in,
    mesh_slope, mesh_grad, own_grad, enc_delta, grid_out, result,
    part, part_out, pair_in, quarter, quarter_out, ens_in, summed, summed_out, z_in, final, final_out,
    in_sem, out_sem, halo_send, halo_recv, a_send, a_recv, b_send, b_recv, c_send, c_recv, d_send, d_recv,
):
    me = lax.axis_index("grid")
    ens = lax.axis_index("ens")
    core = lax.rem(me, 2)
    level = me // 2
    levels = bands // 2
    rows = mesh.shape[0]
    total = x.shape[0]
    blocks = total // rows
    step = total // CHUNKS
    width = x.shape[1]
    far = 2 * core - 1
    far_there = (me + far >= 0) & (me + far < bands)

    def both(act):
        pl.when(far_there)(lambda: act(far))
        act(-far)

    def local(src, dst, sem):
        copy = pltpu.make_async_copy(src, dst, sem)
        copy.start()
        return copy

    targets_copy = local(targets_h, targets, in_sem.at[7])
    edge_copy = local(edge_h, edge, in_sem.at[0])
    enc_copy = local(enc_w_h, enc_w, in_sem.at[1])
    x_copies = [
        local(x_h.at[0, pl.ds(i * step, step)], x.at[pl.ds(i * step, step)], in_sem.at[8 + i])
        for i in range(CHUNKS)
    ]
    agg_copy = local(agg_w_h, agg_w, in_sem.at[2])
    mesh_copy = local(mesh_h.at[0], mesh, in_sem.at[3])
    mweight_copy = local(mweight_h.at[0], mweight, in_sem.at[4])
    proc_copy = local(proc_w_h, proc_w, in_sem.at[5])
    cot_copy = local(cot_h.at[0], cot, in_sem.at[6])
    sources_copy = local(sources_h, sources, in_sem.at[8 + CHUNKS])

    barrier = pltpu.get_barrier_semaphore()

    def greet(**where):
        pl.semaphore_signal(barrier, inc=1, device_id=where, device_id_type=MESH)

    both(lambda off: greet(grid=me + off))
    expected = 1 + far_there.astype(jnp.int32)
    if fused:
        for d in range(1, members):
            greet(ens=lax.rem(ens + d, members))
        for d in range(1, levels):
            greet(grid=lax.rem(level + d, levels) * 2 + core)
        expected = expected + (members - 1) + (levels - 1)

    @pl.when(jnp.logical_not(far_there))
    def clear():
        slot = (1 + far) // 2
        for ref in (panel_in, upd_in, push_in, agg_in):
            ref[slot] = jnp.zeros(ref.shape[1:], ref.dtype)

    targets_copy.wait()
    edge_copy.wait()
    for b in range(blocks):
        first = edge[b, 0].astype(F32)
        second = edge[b, 1].astype(F32)
        for j in range(3):
            hit = [jnp.where(targets[k, b] - me + 1 == j, 1.0, 0.0).astype(F32) for k in range(2)]
            wide[j * rows:(j + 1) * rows, b * rows:(b + 1) * rows] = (first * hit[0] + second * hit[1]).astype(BF16)

    half = width // HALVES
    cols = [slice(h * half, (h + 1) * half) for h in range(HALVES)]

    def halo(turn, h, source, landing, off):
        slot = (1 - off) // 2
        return pltpu.make_async_remote_copy(
            src_ref=source.at[:, cols[h]],
            dst_ref=landing.at[slot, :, cols[h]],
            send_sem=halo_send.at[turn, slot, h],
            recv_sem=halo_recv.at[turn, slot, h],
            device_id={"grid": me + off},
            device_id_type=MESH,
        )

    def received(turn, h, landing):
        act = lambda off: halo(turn, h, landing.at[(1 - off) // 2], landing, off).wait_recv()
        act(far)
        pl.when(far_there)(lambda: act(-far))

    def sent(turn, h, landing):
        both(lambda off: halo(turn, h, landing.at[(1 - off) // 2], landing, off).wait_send())

    enc_copy.wait()
    for h in range(HALVES):
        for i in range(CHUNKS):
            if h == 0:
                x_copies[i].wait()
            span = pl.ds(i * step, step)
            value = dot(x[span], enc_w[:, cols[h]])
            encoded[span, cols[h]] = value
            message = (value * sigmoid(value)).astype(BF16)
            term = dot(wide[:, i * step:(i + 1) * step], message)
            panels[:, cols[h]] = term if i == 0 else panels[:, cols[h]] + term
        if h == 0:
            pl.semaphore_wait(barrier, expected)
        for off in (far, -far):
            panel_out[(1 - off) // 2, :, cols[h]] = panels[pl.ds((1 + off) * rows, rows), cols[h]].astype(BF16)
        both(lambda off: halo(0, h, panel_out.at[(1 - off) // 2], panel_in, off).start())

    def slopes(i, carry):
        span = pl.ds(pl.multiple_of(i * 64, 64), 64)
        encoded[span] = slope_of(encoded[span])
        return carry

    lax.fori_loop(0, total // 64, slopes, 0)
    sources_copy.wait()
    mweight_copy.wait()
    first = mweight[0].astype(F32)
    second = mweight[1].astype(F32)
    for j in range(3):
        hit = [jnp.where(sources[0, k] - me + 1 == j, 1.0, 0.0).astype(F32) for k in range(2)]
        mixed = (first * hit[0] + second * hit[1]).astype(BF16)
        near[j] = mixed
        near_t[j] = mixed.T
    mesh_copy.wait()
    agg_copy.wait()

    partial = [0.0] * HALVES
    for h in range(HALVES):
        received(0, h, panel_in)
        landed = panels[rows:2 * rows, cols[h]]
        for slot in range(2):
            landed = landed + panel_in[slot, :, cols[h]].astype(F32)
        landed = landed.astype(BF16)
        for n in range(HALVES):
            partial[n] = partial[n] + dot(landed, agg_w[cols[h], cols[n]])
            if h == HALVES - 1:
                pre = partial[n]
                sig = sigmoid(pre)
                upd[:, cols[n]] = (mesh[:, cols[n]].astype(F32) + pre * sig).astype(BF16)
                both(lambda off: halo(1, n, upd, upd_in, off).start())
                mesh_slope[:, cols[n]] = sig * (1.0 + pre * (1.0 - sig))

    own = dot(near[1], upd[...])

    def turn_edges(b, carry):
        span = pl.ds(pl.multiple_of(b * rows, rows), rows)
        wide_own_t[span] = wide[rows:2 * rows, span].T
        wide_side_t[span, 0:rows] = wide[0:rows, span].T
        wide_side_t[span, rows:2 * rows] = wide[2 * rows:3 * rows, span].T
        return carry

    deep = width // CHUNKS

    def turn_x(i):
        def body(b, carry):
            span = pl.ds(pl.multiple_of(b * rows, rows), rows)
            x_t[i, :, span] = x[span, i * deep:(i + 1) * deep].T
            return carry

        lax.fori_loop(0, blocks, body, 0)

    lax.fori_loop(0, blocks, turn_edges, 0)
    turn_x(0)
    proc_copy.wait()
    cot_copy.wait()

    proc_pre = 0.0
    for h in range(HALVES):
        received(1, h, upd_in)
        mixed = own[:, cols[h]] + dot(near[0], upd_in[0, :, cols[h]]) + dot(near[2], upd_in[1, :, cols[h]])
        proc_pre = proc_pre + dot(mixed.astype(BF16), proc_w[cols[h], :])
    proc_sig = sigmoid(proc_pre)
    proc_slope = proc_sig * (1.0 + proc_pre * (1.0 - proc_sig))
    upstream = cot[...].astype(F32)
    proc_delta = (upstream * proc_slope).astype(BF16)
    backs = []
    for n in range(HALVES):
        back = dot_t(proc_delta, proc_w[cols[n], :]).astype(BF16)
        for off in (far, -far):
            push_out[(1 - off) // 2, :, cols[n]] = dot(near_t[1 + off], back).astype(BF16)
        both(lambda off: halo(2, n, push_out.at[(1 - off) // 2], push_in, off).start())
        backs.append(back)
    for n in range(HALVES):
        mesh_grad[:, cols[n]] = upstream[:, cols[n]] + dot(near_t[1], backs[n])
    result[...] = (upd[...].astype(F32) + proc_pre * proc_sig).astype(BF16)
    result_copy = local(result, result_h.at[0], out_sem.at[CHUNKS])
    turn_x(1)
    turn_x(2)

    partial = [0.0] * HALVES
    for h in range(HALVES):
        received(2, h, push_in)
        landed = mesh_grad[:, cols[h]]
        for slot in range(2):
            landed = landed + push_in[slot, :, cols[h]].astype(F32)
        landed = (landed * mesh_slope[:, cols[h]]).astype(BF16)
        for n in range(HALVES):
            partial[n] = partial[n] + dot_t(landed, agg_w[cols[n], cols[h]])
            if h == HALVES - 1:
                agg[:, cols[n]] = partial[n].astype(BF16)
                both(lambda off: halo(3, n, agg, agg_in, off).start())

    def own_part(i, carry):
        span = pl.ds(pl.multiple_of(i * step, step), step)
        own_grad[span] = dot(wide_own_t[span], agg[...])
        return carry

    lax.fori_loop(0, CHUNKS, own_part, 0)
    turn_x(3)

    for h in range(HALVES):
        received(3, h, agg_in)
        sides = agg_in[:, :, cols[h]].reshape(2 * rows, half)
        for i in range(CHUNKS):
            span = pl.ds(i * step, step)
            grad = own_grad[span, cols[h]] + dot(wide_side_t[span], sides)
            enc_delta[span, cols[h]] = (grad * encoded[span, cols[h]]).astype(BF16)

    def grid_part(i):
        span = pl.ds(i * step, step)
        grid_out[span] = dot_t(enc_delta[span], enc_w[...]).astype(BF16)
        return local(grid_out.at[span], grid_h.at[0, span], out_sem.at[i])

    if not fused:
        for i in range(CHUNKS):
            part[i] = dot(x_t[i], enc_delta[...]) * scale
        final_copy = local(part, final_h, out_sem.at[CHUNKS + 1])
        grid_copies = [grid_part(i) for i in range(CHUNKS)]
    else:
        share = part.shape[2]
        mine = share // members

        def pair(z):
            return pltpu.make_async_remote_copy(
                src_ref=part_out.at[z, 1 - core], dst_ref=pair_in.at[z],
                send_sem=a_send.at[z], recv_sem=a_recv.at[z],
                device_id={"grid": me + 1 - 2 * core}, device_id_type=MESH)

        def across(z, d, arriving):
            peer = lax.rem(ens + d, members)
            slot = peer if arriving else ens
            return pltpu.make_async_remote_copy(
                src_ref=quarter_out.at[z, peer], dst_ref=ens_in.at[z, slot],
                send_sem=b_send.at[z, peer], recv_sem=b_recv.at[z, slot],
                device_id={"ens": peer}, device_id_type=MESH)

        def along(d, arriving):
            peer = lax.rem(level + d, levels)
            slot = peer if arriving else level
            return pltpu.make_async_remote_copy(
                src_ref=summed_out.at[peer], dst_ref=z_in.at[slot],
                send_sem=c_send.at[peer], recv_sem=c_recv.at[slot],
                device_id={"grid": peer * 2 + core}, device_id_type=MESH)

        def gather(d, arriving):
            peer = lax.rem(ens + d, members)
            slot = peer if arriving else ens
            return pltpu.make_async_remote_copy(
                src_ref=final.at[ens], dst_ref=final.at[slot],
                send_sem=d_send.at[peer], recv_sem=d_recv.at[slot],
                device_id={"ens": peer}, device_id_type=MESH)

        order = [lax.rem(level + d, levels) for d in list(range(1, levels)) + [0]]
        for z in order:
            value = (dot(x_t[z], enc_delta[...]) * scale).reshape(2, share, width)
            part[z] = value
            part_out[z] = value.astype(BF16)
            pair(z).start()
        grid_copies = [grid_part(0)]
        for z in order:
            pair(z).wait_recv()
            value = part[z, core] + pair_in[z].astype(F32)
            value = value.reshape(members, mine, width)
            quarter[z] = value
            quarter_out[z] = value.astype(BF16)
            for d in range(1, members):
                across(z, d, False).start()
        grid_copies += [grid_part(i) for i in range(1, CHUNKS)]
        for n, z in enumerate(order):
            value = quarter[z, ens]
            for d in range(1, members):
                across(z, d, True).wait_recv()
                value = value + ens_in[z, lax.rem(ens + d, members)].astype(F32)
            if n < levels - 1:
                summed_out[z] = value.astype(BF16)
                along(n + 1, False).start()
            else:
                summed[...] = value
        value = summed[...]
        for d in range(1, levels):
            along(d, True).wait_recv()
            value = value + z_in[lax.rem(level + d, levels)].astype(F32)
        final[ens] = value.astype(BF16)
        for d in range(1, members):
            gather(d, False).start()
        for d in range(1, members):
            gather(d, True).wait_recv()
        final_out[...] = final[...].astype(F32)
        final_copy = local(final_out, final_h, out_sem.at[CHUNKS + 1])
        for z in order:
            pair(z).wait_send()
            for d in range(1, members):
                across(z, d, False).wait_send()
        for d in range(1, levels):
            along(d, False).wait_send()
        for d in range(1, members):
            gather(d, False).wait_send()

    for turn, landing in enumerate((panel_in, upd_in, push_in, agg_in)):
        for h in range(HALVES):
            sent(turn, h, landing)
    result_copy.wait()
    for copy in grid_copies:
        copy.wait()
    final_copy.wait()


def leave(result, grid_grad, grad, result_out, grid_out, grad_out, one, two, three, in_sem, out_sem):
    step = grid_grad.shape[1] // CHUNKS
    moves = [(result, one, result_out), (grad, three, grad_out)]
    for i in range(CHUNKS):
        span = pl.ds(i * step, step)
        moves.append((grid_grad.at[:, span], two.at[:, span], grid_out.at[:, span]))
    arriving = [pltpu.make_async_copy(a, b, in_sem.at[i]) for i, (a, b, c) in enumerate(moves)]
    leaving = [pltpu.make_async_copy(b, c, out_sem.at[i]) for i, (a, b, c) in enumerate(moves)]
    for copy in arriving:
        copy.start()
    for first, second in zip(arriving, leaving):
        first.wait()
        second.start()
    for copy in leaving:
        copy.wait()


def on_device(
    bands, members,
    grid_latent, mesh_latent, cotangent, edge_weights, edge_targets, mesh_weights, mesh_sources,
    encode_weight, aggregate_weight, process_weight,
):
    unused, total, width = grid_latent.shape
    rows = mesh_latent.shape[1]
    share = width // bands
    levels = max(bands // 2, 1)
    fused = bands % 2 == 0 and levels == CHUNKS and share % (16 * members) == 0
    scale = 1.0 / float(members * total * bands) ** 0.5
    mine = share // members if fused else 16
    gshape = (CHUNKS, 2, width // CHUNKS // 2, width) if fused else (CHUNKS, width // CHUNKS, width)
    last = (members, mine, width) if fused else gshape
    vm = pltpu.VMEM
    dma = pltpu.SemaphoreType.DMA
    panel = (2, rows, width)
    quarters = (CHUNKS, members, mine, width)
    scratch = [
        vm((total, width), BF16), vm((rows, width), BF16), vm((rows, width), BF16),
        vm(edge_weights.shape, BF16),
        pltpu.SMEM(edge_targets.shape[::-1], jnp.int32), vm(mesh_weights.shape[1:], BF16),
        pltpu.SMEM(mesh_sources.shape, jnp.int32),
        vm((width, width), BF16), vm((width, width), BF16), vm((width, width), BF16),
        vm((3 * rows, total), BF16), vm((total, rows), BF16), vm((total, 2 * rows), BF16),
        vm((3, rows, rows), BF16), vm((3, rows, rows), BF16), vm((CHUNKS, width // CHUNKS, total), BF16),
        vm((total, width), F32), vm((3 * rows, width), F32),
        vm(panel, BF16), vm(panel, BF16), vm((rows, width), BF16), vm(panel, BF16),
        vm(panel, BF16), vm(panel, BF16), vm((rows, width), BF16), vm(panel, BF16),
        vm((rows, width), F32), vm((rows, width), F32),
        vm((total, width), F32), vm((total, width), BF16), vm((total, width), BF16), vm((rows, width), BF16),
        vm(gshape, F32), vm(gshape, BF16), vm((CHUNKS, width // CHUNKS // 2, width), BF16),
        vm(quarters, F32), vm(quarters, BF16), vm(quarters, BF16),
        vm((mine, width), F32), vm((CHUNKS, mine, width), BF16), vm((CHUNKS, mine, width), BF16),
        vm((members, mine, width), BF16), vm((members, mine, width), F32),
        dma((9 + CHUNKS,)), dma((CHUNKS + 2,)), dma((4, 2, HALVES)), dma((4, 2, HALVES)),
        dma((CHUNKS,)), dma((CHUNKS,)), dma((CHUNKS, members)), dma((CHUNKS, members)),
        dma((CHUNKS,)), dma((CHUNKS,)), dma((members,)), dma((members,)),
    ]
    hbm = pl.BlockSpec(memory_space=pltpu.HBM)
    anywhere = pl.BlockSpec(memory_space=pl.ANY)
    result, grid_grad, grad = pl.pallas_call(
        functools.partial(kernel, bands, members, scale, fused),
        out_shape=(
            jax.ShapeDtypeStruct(mesh_latent.shape, BF16),
            jax.ShapeDtypeStruct(grid_latent.shape, BF16),
            jax.ShapeDtypeStruct(last, F32),
        ),
        in_specs=[hbm] * 10,
        out_specs=(anywhere,) * 3,
        scratch_shapes=scratch,
        compiler_params=pltpu.CompilerParams(
            collective_id=0, has_side_effects=True, vmem_limit_bytes=63 * 1024 * 1024
        ),
    )(
        grid_latent, mesh_latent, cotangent, edge_weights, edge_targets.T, mesh_weights, mesh_sources,
        encode_weight, aggregate_weight, process_weight,
    )
    if fused:
        result, grid_grad, grad = pl.pallas_call(
            leave,
            out_shape=tuple(jax.ShapeDtypeStruct(a.shape, a.dtype) for a in (result, grid_grad, grad)),
            in_specs=[anywhere] * 3,
            out_specs=(hbm,) * 3,
            scratch_shapes=[vm(a.shape, a.dtype) for a in (result, grid_grad, grad)] + [dma((2 + CHUNKS,))] * 2,
            compiler_params=pltpu.CompilerParams(vmem_limit_bytes=63 * 1024 * 1024),
        )(result, grid_grad, grad)
        grad = grad.reshape(share, width)
    else:
        summed = lax.psum(grad.reshape(width, width), ("ens", "grid"))
        grad = lax.dynamic_slice_in_dim(summed, lax.axis_index("grid") * share, share, 0)
    return result, grid_grad, grad


def solution(mesh):
    return jax.shard_map(
        functools.partial(on_device, mesh.shape["grid"], mesh.shape["ens"]),
        mesh=mesh,
        in_specs=(
            P("ens", "grid", None),
            P("ens", "grid", None),
            P("ens", "grid", None),
            P("grid", None, None, None),
            P("grid", None),
            P("grid", None, None, None),
            P("grid", None),
            P(),
            P(),
            P(),
        ),
        out_specs=(P("ens", "grid", None), P("ens", "grid", None), P("grid", None)),
        check_vma=False,
    )
```

```python
import functools

import jax
import jax.numpy as jnp
from jax import lax
from jax.experimental import pallas as pl
from jax.experimental.pallas import tpu as pltpu
from jax.sharding import PartitionSpec as P

MESH = pl.DeviceIdType.MESH
F32 = jnp.float32
BF16 = jnp.bfloat16
CHUNKS = 4
HALVES = 2


def sigmoid(value):
    return 0.5 + 0.5 * jnp.tanh(0.5 * value)


def slope_of(value):
    sig = sigmoid(value)
    return sig * (1.0 + value * (1.0 - sig))


def dot(a, b):
    return jnp.dot(a, b, preferred_element_type=F32)


def dot_t(a, b):
    return lax.dot_general(a, b, (((1,), (1,)), ((), ())), preferred_element_type=F32)


def kernel(
    bands, members, scale, fused,
    x_h, mesh_h, cot_h, edge_h, targets_h, mweight_h, sources_h, enc_w_h, agg_w_h, proc_w_h,
    result_h, grid_h, final_h,
    x, mesh, cot, edge, targets, mweight, sources, enc_w, agg_w, proc_w,
    wide, wide_own_t, wide_side_t, near, near_t, x_t,
    encoded, panels, panel_out, panel_in, upd, upd_in, push_out, push_in, agg, agg_in,
    mesh_slope, mesh_grad, own_grad, enc_delta, grid_out, result,
    part, part_out, pair_in, quarter, quarter_out, ens_in, summed, summed_out, z_in, final, final_out,
    in_sem, out_sem, halo_send, halo_recv, a_send, a_recv, b_send, b_recv, c_send, c_recv, d_send, d_recv,
):
    me = lax.axis_index("grid")
    ens = lax.axis_index("ens")
    core = lax.rem(me, 2)
    level = me // 2
    levels = bands // 2
    rows = mesh.shape[0]
    total = x.shape[0]
    blocks = total // rows
    step = total // CHUNKS
    width = x.shape[1]
    far = 2 * core - 1
    far_there = (me + far >= 0) & (me + far < bands)

    def both(act):
        pl.when(far_there)(lambda: act(far))
        act(-far)

    def local(src, dst, sem):
        copy = pltpu.make_async_copy(src, dst, sem)
        copy.start()
        return copy

    targets_copy = local(targets_h, targets, in_sem.at[7])
    edge_copy = local(edge_h, edge, in_sem.at[0])
    enc_copy = local(enc_w_h, enc_w, in_sem.at[1])
    x_copies = [
        local(x_h.at[0, pl.ds(i * step, step)], x.at[pl.ds(i * step, step)], in_sem.at[8 + i])
        for i in range(CHUNKS)
    ]
    agg_copy = local(agg_w_h, agg_w, in_sem.at[2])
    mesh_copy = local(mesh_h.at[0], mesh, in_sem.at[3])
    mweight_copy = local(mweight_h.at[0], mweight, in_sem.at[4])
    proc_copy = local(proc_w_h, proc_w, in_sem.at[5])
    cot_copy = local(cot_h.at[0], cot, in_sem.at[6])
    sources_copy = local(sources_h, sources, in_sem.at[8 + CHUNKS])

    barrier = pltpu.get_barrier_semaphore()

    def greet(**where):
        pl.semaphore_signal(barrier, inc=1, device_id=where, device_id_type=MESH)

    both(lambda off: greet(grid=me + off))
    expected = 1 + far_there.astype(jnp.int32)
    if fused:
        for d in range(1, members):
            greet(ens=lax.rem(ens + d, members))
        for d in range(1, levels):
            greet(grid=lax.rem(level + d, levels) * 2 + core)
        expected = expected + (members - 1) + (levels - 1)

    @pl.when(jnp.logical_not(far_there))
    def clear():
        slot = (1 + far) // 2
        for ref in (panel_in, upd_in, push_in, agg_in):
            ref[slot] = jnp.zeros(ref.shape[1:], ref.dtype)

    targets_copy.wait()
    edge_copy.wait()

    def mix_edges(b, carry):
        first = edge[b, 0].astype(F32)
        second = edge[b, 1].astype(F32)
        span = pl.ds(pl.multiple_of(b * rows, rows), rows)
        for j in range(3):
            hit = [jnp.where(targets[k, b] - me + 1 == j, 1.0, 0.0).astype(F32) for k in range(2)]
            wide[j * rows:(j + 1) * rows, span] = (first * hit[0] + second * hit[1]).astype(BF16)
        return carry

    lax.fori_loop(0, blocks, mix_edges, 0)
    panels[...] = jnp.zeros_like(panels)

    half = width // HALVES
    cols = [slice(h * half, (h + 1) * half) for h in range(HALVES)]

    def halo(turn, h, source, landing, off):
        slot = (1 - off) // 2
        return pltpu.make_async_remote_copy(
            src_ref=source.at[:, cols[h]],
            dst_ref=landing.at[slot, :, cols[h]],
            send_sem=halo_send.at[turn, slot, h],
            recv_sem=halo_recv.at[turn, slot, h],
            device_id={"grid": me + off},
            device_id_type=MESH,
        )

    def received(turn, h, landing):
        act = lambda off: halo(turn, h, landing.at[(1 - off) // 2], landing, off).wait_recv()
        act(far)
        pl.when(far_there)(lambda: act(-far))

    def sent(turn, h, landing):
        both(lambda off: halo(turn, h, landing.at[(1 - off) // 2], landing, off).wait_send())

    enc_copy.wait()
    for h in range(HALVES):
        if h == 0:
            for copy in x_copies:
                copy.wait()

        def encode(i, carry):
            span = pl.ds(pl.multiple_of(i * step, step), step)
            value = dot(x[span], enc_w[:, cols[h]])
            encoded[span, cols[h]] = value
            message = (value * sigmoid(value)).astype(BF16)
            panels[:, cols[h]] += dot(wide[:, span], message)
            return carry

        lax.fori_loop(0, CHUNKS, encode, 0)
        if h == 0:
            pl.semaphore_wait(barrier, expected)
        for off in (far, -far):
            panel_out[(1 - off) // 2, :, cols[h]] = panels[pl.ds((1 + off) * rows, rows), cols[h]].astype(BF16)
        both(lambda off: halo(0, h, panel_out.at[(1 - off) // 2], panel_in, off).start())

    def slopes(i, carry):
        span = pl.ds(pl.multiple_of(i * 64, 64), 64)
        encoded[span] = slope_of(encoded[span])
        return carry

    lax.fori_loop(0, total // 64, slopes, 0)
    sources_copy.wait()
    mweight_copy.wait()
    first = mweight[0].astype(F32)
    second = mweight[1].astype(F32)
    for j in range(3):
        hit = [jnp.where(sources[0, k] - me + 1 == j, 1.0, 0.0).astype(F32) for k in range(2)]
        mixed = (first * hit[0] + second * hit[1]).astype(BF16)
        near[j] = mixed
        near_t[j] = mixed.T
    mesh_copy.wait()
    agg_copy.wait()

    partial = [0.0] * HALVES
    for h in range(HALVES):
        received(0, h, panel_in)
        landed = panels[rows:2 * rows, cols[h]]
        for slot in range(2):
            landed = landed + panel_in[slot, :, cols[h]].astype(F32)
        landed = landed.astype(BF16)
        for n in range(HALVES):
            partial[n] = partial[n] + dot(landed, agg_w[cols[h], cols[n]])
            if h == HALVES - 1:
                pre = partial[n]
                sig = sigmoid(pre)
                upd[:, cols[n]] = (mesh[:, cols[n]].astype(F32) + pre * sig).astype(BF16)
                both(lambda off: halo(1, n, upd, upd_in, off).start())
                mesh_slope[:, cols[n]] = sig * (1.0 + pre * (1.0 - sig))

    own = dot(near[1], upd[...])

    def turn_edges(b, carry):
        span = pl.ds(pl.multiple_of(b * rows, rows), rows)
        wide_own_t[span] = wide[rows:2 * rows, span].T
        wide_side_t[span, 0:rows] = wide[0:rows, span].T
        wide_side_t[span, rows:2 * rows] = wide[2 * rows:3 * rows, span].T
        return carry

    deep = width // CHUNKS

    def turn_x(i):
        def body(b, carry):
            span = pl.ds(pl.multiple_of(b * rows, rows), rows)
            x_t[i, :, span] = x[span, i * deep:(i + 1) * deep].T
            return carry

        lax.fori_loop(0, blocks, body, 0)

    lax.fori_loop(0, blocks, turn_edges, 0)
    turn_x(0)
    proc_copy.wait()
    cot_copy.wait()

    proc_pre = 0.0
    for h in range(HALVES):
        received(1, h, upd_in)
        mixed = own[:, cols[h]] + dot(near[0], upd_in[0, :, cols[h]]) + dot(near[2], upd_in[1, :, cols[h]])
        proc_pre = proc_pre + dot(mixed.astype(BF16), proc_w[cols[h], :])
    proc_sig = sigmoid(proc_pre)
    proc_slope = proc_sig * (1.0 + proc_pre * (1.0 - proc_sig))
    upstream = cot[...].astype(F32)
    proc_delta = (upstream * proc_slope).astype(BF16)
    backs = []
    for n in range(HALVES):
        back = dot_t(proc_delta, proc_w[cols[n], :]).astype(BF16)
        for off in (far, -far):
            push_out[(1 - off) // 2, :, cols[n]] = dot(near_t[1 + off], back).astype(BF16)
        both(lambda off: halo(2, n, push_out.at[(1 - off) // 2], push_in, off).start())
        backs.append(back)
    for n in range(HALVES):
        mesh_grad[:, cols[n]] = upstream[:, cols[n]] + dot(near_t[1], backs[n])
    result[...] = (upd[...].astype(F32) + proc_pre * proc_sig).astype(BF16)
    result_copy = local(result, result_h.at[0], out_sem.at[CHUNKS])
    turn_x(1)
    turn_x(2)

    partial = [0.0] * HALVES
    for h in range(HALVES):
        received(2, h, push_in)
        landed = mesh_grad[:, cols[h]]
        for slot in range(2):
            landed = landed + push_in[slot, :, cols[h]].astype(F32)
        landed = (landed * mesh_slope[:, cols[h]]).astype(BF16)
        for n in range(HALVES):
            partial[n] = partial[n] + dot_t(landed, agg_w[cols[n], cols[h]])
            if h == HALVES - 1:
                agg[:, cols[n]] = partial[n].astype(BF16)
                both(lambda off: halo(3, n, agg, agg_in, off).start())

    def own_part(i, carry):
        span = pl.ds(pl.multiple_of(i * step, step), step)
        own_grad[span] = dot(wide_own_t[span], agg[...])
        return carry

    lax.fori_loop(0, CHUNKS, own_part, 0)
    turn_x(3)

    for h in range(HALVES):
        received(3, h, agg_in)
        sides = agg_in[:, :, cols[h]].reshape(2 * rows, half)

        def deltas(i, carry):
            span = pl.ds(pl.multiple_of(i * step, step), step)
            grad = own_grad[span, cols[h]] + dot(wide_side_t[span], sides)
            enc_delta[span, cols[h]] = (grad * encoded[span, cols[h]]).astype(BF16)
            return carry

        lax.fori_loop(0, CHUNKS, deltas, 0)

    def grid_copy(i):
        span = pl.ds(pl.multiple_of(i * step, step), step)
        return pltpu.make_async_copy(grid_out.at[span], grid_h.at[0, span], out_sem.at[i])

    def grid_part(i, carry):
        span = pl.ds(pl.multiple_of(i * step, step), step)
        grid_out[span] = dot_t(enc_delta[span], enc_w[...]).astype(BF16)
        grid_copy(i).start()
        return carry

    if not fused:
        for i in range(CHUNKS):
            part[i] = dot(x_t[i], enc_delta[...]) * scale
        final_copy = local(part, final_h, out_sem.at[CHUNKS + 1])
        lax.fori_loop(0, CHUNKS, grid_part, 0)
    else:
        share = part.shape[2]
        mine = share // members

        def pair(z):
            return pltpu.make_async_remote_copy(
                src_ref=part_out.at[z, 1 - core], dst_ref=pair_in.at[z],
                send_sem=a_send.at[z], recv_sem=a_recv.at[z],
                device_id={"grid": me + 1 - 2 * core}, device_id_type=MESH)

        def across(z, d, arriving):
            peer = lax.rem(ens + d, members)
            slot = peer if arriving else ens
            return pltpu.make_async_remote_copy(
                src_ref=quarter_out.at[z, peer], dst_ref=ens_in.at[z, slot],
                send_sem=b_send.at[z, peer], recv_sem=b_recv.at[z, slot],
                device_id={"ens": peer}, device_id_type=MESH)

        def along(d, arriving):
            peer = lax.rem(level + d, levels)
            slot = peer if arriving else level
            return pltpu.make_async_remote_copy(
                src_ref=summed_out.at[peer], dst_ref=z_in.at[slot],
                send_sem=c_send.at[peer], recv_sem=c_recv.at[slot],
                device_id={"grid": peer * 2 + core}, device_id_type=MESH)

        def gather(d, arriving):
            peer = lax.rem(ens + d, members)
            slot = peer if arriving else ens
            return pltpu.make_async_remote_copy(
                src_ref=final.at[ens], dst_ref=final.at[slot],
                send_sem=d_send.at[peer], recv_sem=d_recv.at[slot],
                device_id={"ens": peer}, device_id_type=MESH)

        order = [lax.rem(level + d, levels) for d in list(range(1, levels)) + [0]]

        def weigh(n, carry):
            z = lax.rem(level + 1 + n, levels)
            value = (dot(x_t[z], enc_delta[...]) * scale).reshape(2, share, width)
            part[z] = value
            part_out[z] = value.astype(BF16)
            pair(z).start()
            return carry

        def pair_up(n, carry):
            z = lax.rem(level + 1 + n, levels)
            pair(z).wait_recv()
            value = part[z, core] + pair_in[z].astype(F32)
            value = value.reshape(members, mine, width)
            quarter[z] = value
            quarter_out[z] = value.astype(BF16)
            for d in range(1, members):
                across(z, d, False).start()
            return carry

        def add_up(z):
            value = quarter[z, ens]
            for d in range(1, members):
                across(z, d, True).wait_recv()
                value = value + ens_in[z, lax.rem(ens + d, members)].astype(F32)
            return value

        def pass_on(n, carry):
            z = lax.rem(level + n, levels)
            summed_out[z] = add_up(z).astype(BF16)
            along(n, False).start()
            return carry

        lax.fori_loop(0, levels, weigh, 0)
        lax.fori_loop(0, levels, pair_up, 0)
        lax.fori_loop(0, CHUNKS, grid_part, 0)
        lax.fori_loop(1, levels, pass_on, 0)
        summed[...] = add_up(level)
        value = summed[...]
        for d in range(1, levels):
            along(d, True).wait_recv()
            value = value + z_in[lax.rem(level + d, levels)].astype(F32)
        final[ens] = value.astype(BF16)
        for d in range(1, members):
            gather(d, False).start()
        for d in range(1, members):
            gather(d, True).wait_recv()
        final_out[...] = final[...].astype(F32)
        final_copy = local(final_out, final_h, out_sem.at[CHUNKS + 1])
        for z in order:
            pair(z).wait_send()
            for d in range(1, members):
                across(z, d, False).wait_send()
        for d in range(1, levels):
            along(d, False).wait_send()
        for d in range(1, members):
            gather(d, False).wait_send()

    for turn, landing in enumerate((panel_in, upd_in, push_in, agg_in)):
        for h in range(HALVES):
            sent(turn, h, landing)
    result_copy.wait()
    for i in range(CHUNKS):
        grid_copy(i).wait()
    final_copy.wait()


def leave(result, grid_grad, grad, result_out, grid_out, grad_out, one, two, three, in_sem, out_sem):
    step = grid_grad.shape[1] // CHUNKS
    moves = [(result, one, result_out), (grad, three, grad_out)]
    for i in range(CHUNKS):
        span = pl.ds(i * step, step)
        moves.append((grid_grad.at[:, span], two.at[:, span], grid_out.at[:, span]))
    arriving = [pltpu.make_async_copy(a, b, in_sem.at[i]) for i, (a, b, c) in enumerate(moves)]
    leaving = [pltpu.make_async_copy(b, c, out_sem.at[i]) for i, (a, b, c) in enumerate(moves)]
    for copy in arriving:
        copy.start()
    for first, second in zip(arriving, leaving):
        first.wait()
        second.start()
    for copy in leaving:
        copy.wait()


def on_device(
    bands, members,
    grid_latent, mesh_latent, cotangent, edge_weights, edge_targets, mesh_weights, mesh_sources,
    encode_weight, aggregate_weight, process_weight,
):
    unused, total, width = grid_latent.shape
    rows = mesh_latent.shape[1]
    share = width // bands
    levels = max(bands // 2, 1)
    fused = bands % 2 == 0 and levels == CHUNKS and share % (16 * members) == 0
    scale = 1.0 / float(members * total * bands) ** 0.5
    mine = share // members if fused else 16
    gshape = (CHUNKS, 2, width // CHUNKS // 2, width) if fused else (CHUNKS, width // CHUNKS, width)
    last = (members, mine, width) if fused else gshape
    vm = pltpu.VMEM
    dma = pltpu.SemaphoreType.DMA
    panel = (2, rows, width)
    quarters = (CHUNKS, members, mine, width)
    scratch = [
        vm((total, width), BF16), vm((rows, width), BF16), vm((rows, width), BF16),
        vm(edge_weights.shape, BF16),
        pltpu.SMEM(edge_targets.shape[::-1], jnp.int32), vm(mesh_weights.shape[1:], BF16),
        pltpu.SMEM(mesh_sources.shape, jnp.int32),
        vm((width, width), BF16), vm((width, width), BF16), vm((width, width), BF16),
        vm((3 * rows, total), BF16), vm((total, rows), BF16), vm((total, 2 * rows), BF16),
        vm((3, rows, rows), BF16), vm((3, rows, rows), BF16), vm((CHUNKS, width // CHUNKS, total), BF16),
        vm((total, width), F32), vm((3 * rows, width), F32),
        vm(panel, BF16), vm(panel, BF16), vm((rows, width), BF16), vm(panel, BF16),
        vm(panel, BF16), vm(panel, BF16), vm((rows, width), BF16), vm(panel, BF16),
        vm((rows, width), F32), vm((rows, width), F32),
        vm((total, width), F32), vm((total, width), BF16), vm((total, width), BF16), vm((rows, width), BF16),
        vm(gshape, F32), vm(gshape, BF16), vm((CHUNKS, width // CHUNKS // 2, width), BF16),
        vm(quarters, F32), vm(quarters, BF16), vm(quarters, BF16),
        vm((mine, width), F32), vm((CHUNKS, mine, width), BF16), vm((CHUNKS, mine, width), BF16),
        vm((members, mine, width), BF16), vm((members, mine, width), F32),
        dma((9 + CHUNKS,)), dma((CHUNKS + 2,)), dma((4, 2, HALVES)), dma((4, 2, HALVES)),
        dma((CHUNKS,)), dma((CHUNKS,)), dma((CHUNKS, members)), dma((CHUNKS, members)),
        dma((CHUNKS,)), dma((CHUNKS,)), dma((members,)), dma((members,)),
    ]
    hbm = pl.BlockSpec(memory_space=pltpu.HBM)
    anywhere = pl.BlockSpec(memory_space=pl.ANY)
    result, grid_grad, grad = pl.pallas_call(
        functools.partial(kernel, bands, members, scale, fused),
        out_shape=(
            jax.ShapeDtypeStruct(mesh_latent.shape, BF16),
            jax.ShapeDtypeStruct(grid_latent.shape, BF16),
            jax.ShapeDtypeStruct(last, F32),
        ),
        in_specs=[hbm] * 10,
        out_specs=(anywhere,) * 3,
        scratch_shapes=scratch,
        compiler_params=pltpu.CompilerParams(
            collective_id=0, has_side_effects=True, vmem_limit_bytes=63 * 1024 * 1024
        ),
    )(
        grid_latent, mesh_latent, cotangent, edge_weights, edge_targets.T, mesh_weights, mesh_sources,
        encode_weight, aggregate_weight, process_weight,
    )
    if fused:
        result, grid_grad, grad = pl.pallas_call(
            leave,
            out_shape=tuple(jax.ShapeDtypeStruct(a.shape, a.dtype) for a in (result, grid_grad, grad)),
            in_specs=[anywhere] * 3,
            out_specs=(hbm,) * 3,
            scratch_shapes=[vm(a.shape, a.dtype) for a in (result, grid_grad, grad)] + [dma((2 + CHUNKS,))] * 2,
            compiler_params=pltpu.CompilerParams(vmem_limit_bytes=63 * 1024 * 1024),
        )(result, grid_grad, grad)
        grad = grad.reshape(share, width)
    else:
        summed = lax.psum(grad.reshape(width, width), ("ens", "grid"))
        grad = lax.dynamic_slice_in_dim(summed, lax.axis_index("grid") * share, share, 0)
    return result, grid_grad, grad


def solution(mesh):
    return jax.shard_map(
        functools.partial(on_device, mesh.shape["grid"], mesh.shape["ens"]),
        mesh=mesh,
        in_specs=(
            P("ens", "grid", None),
            P("ens", "grid", None),
            P("ens", "grid", None),
            P("grid", None, None, None),
            P("grid", None),
            P("grid", None, None, None),
            P("grid", None),
            P(),
            P(),
            P(),
        ),
        out_specs=(P("ens", "grid", None), P("ens", "grid", None), P("grid", None)),
        check_vma=False,
    )
```

```python
import functools

import jax
import jax.numpy as jnp
from jax import lax
from jax.experimental import pallas as pl
from jax.experimental.pallas import tpu as pltpu
from jax.sharding import PartitionSpec as P

MESH = pl.DeviceIdType.MESH
F32 = jnp.float32
BF16 = jnp.bfloat16
CHUNKS = 4
HALVES = 2


def sigmoid(value):
    return 0.5 + 0.5 * jnp.tanh(0.5 * value)


def dot(a, b):
    return jnp.dot(a, b, preferred_element_type=F32)


def dot_t(a, b):
    return lax.dot_general(a, b, (((1,), (1,)), ((), ())), preferred_element_type=F32)


def kernel(
    bands, members, scale, fused,
    x_h, mesh_h, cot_h, edge_h, targets_h, mweight_h, sources_h, enc_w_h, agg_w_h, proc_w_h,
    result_h, grid_h, final_h,
    x, mesh, cot, edge, targets, mweight, sources, enc_w, agg_w, proc_w,
    wide, wide_own_t, wide_side_t, near, near_t, x_t,
    slopes, panels, panel_out, panel_in, upd, upd_in, push_out, push_in, agg, agg_in,
    mesh_slope, mesh_grad, own_grad, enc_delta, grid_out, result,
    part, part_out, pair_in, quarter, quarter_out, ens_in, summed, summed_out, z_in, final, final_out,
    in_sem, out_sem, halo_send, halo_recv, a_send, a_recv, b_send, b_recv, c_send, c_recv, d_send, d_recv,
):
    me = lax.axis_index("grid")
    ens = lax.axis_index("ens")
    core = lax.rem(me, 2)
    level = me // 2
    levels = bands // 2
    rows = mesh.shape[0]
    total = x.shape[0]
    blocks = total // rows
    step = total // CHUNKS
    width = x.shape[1]
    far = 2 * core - 1
    far_there = (me + far >= 0) & (me + far < bands)

    def both(act):
        pl.when(far_there)(lambda: act(far))
        act(-far)

    def local(src, dst, sem):
        copy = pltpu.make_async_copy(src, dst, sem)
        copy.start()
        return copy

    targets_copy = local(targets_h, targets, in_sem.at[7])
    edge_copy = local(edge_h, edge, in_sem.at[0])
    enc_copy = local(enc_w_h, enc_w, in_sem.at[1])
    x_copies = [
        local(x_h.at[0, pl.ds(i * step, step)], x.at[pl.ds(i * step, step)], in_sem.at[8 + i])
        for i in range(CHUNKS)
    ]
    agg_copy = local(agg_w_h, agg_w, in_sem.at[2])
    mesh_copy = local(mesh_h.at[0], mesh, in_sem.at[3])
    mweight_copy = local(mweight_h.at[0], mweight, in_sem.at[4])
    proc_copy = local(proc_w_h, proc_w, in_sem.at[5])
    cot_copy = local(cot_h.at[0], cot, in_sem.at[6])
    sources_copy = local(sources_h, sources, in_sem.at[8 + CHUNKS])

    barrier = pltpu.get_barrier_semaphore()

    def greet(**where):
        pl.semaphore_signal(barrier, inc=1, device_id=where, device_id_type=MESH)

    both(lambda off: greet(grid=me + off))
    expected = 1 + far_there.astype(jnp.int32)
    if fused:
        for d in range(1, members):
            greet(ens=lax.rem(ens + d, members))
        for d in range(1, levels):
            greet(grid=lax.rem(level + d, levels) * 2 + core)
        expected = expected + (members - 1) + (levels - 1)

    @pl.when(jnp.logical_not(far_there))
    def clear():
        slot = (1 + far) // 2
        for ref in (panel_in, upd_in, push_in, agg_in):
            ref[slot] = jnp.zeros(ref.shape[1:], ref.dtype)

    targets_copy.wait()
    edge_copy.wait()
    for b in range(blocks):
        first = edge[b, 0].astype(F32)
        second = edge[b, 1].astype(F32)
        for j in range(3):
            hit = [jnp.where(targets[k, b] - me + 1 == j, 1.0, 0.0).astype(F32) for k in range(2)]
            wide[j * rows:(j + 1) * rows, b * rows:(b + 1) * rows] = (first * hit[0] + second * hit[1]).astype(BF16)

    half = width // HALVES
    cols = [slice(h * half, (h + 1) * half) for h in range(HALVES)]

    def halo(turn, h, source, landing, off):
        slot = (1 - off) // 2
        return pltpu.make_async_remote_copy(
            src_ref=source.at[:, cols[h]],
            dst_ref=landing.at[slot, :, cols[h]],
            send_sem=halo_send.at[turn, slot, h],
            recv_sem=halo_recv.at[turn, slot, h],
            device_id={"grid": me + off},
            device_id_type=MESH,
        )

    def received(turn, h, landing):
        act = lambda off: halo(turn, h, landing.at[(1 - off) // 2], landing, off).wait_recv()
        act(far)
        pl.when(far_there)(lambda: act(-far))

    def sent(turn, h, landing):
        both(lambda off: halo(turn, h, landing.at[(1 - off) // 2], landing, off).wait_send())

    enc_copy.wait()
    for h in range(HALVES):
        for i in range(CHUNKS):
            if h == 0:
                x_copies[i].wait()
            span = pl.ds(i * step, step)
            value = dot(x[span], enc_w[:, cols[h]])
            sig = sigmoid(value)
            message = value * sig
            slopes[span, cols[h]] = sig + message * (1.0 - sig)
            term = dot(wide[:, i * step:(i + 1) * step], message.astype(BF16))
            panels[:, cols[h]] = term if i == 0 else panels[:, cols[h]] + term
        if h == 0:
            pl.semaphore_wait(barrier, expected)
        for off in (far, -far):
            panel_out[(1 - off) // 2, :, cols[h]] = panels[pl.ds((1 + off) * rows, rows), cols[h]].astype(BF16)
        both(lambda off: halo(0, h, panel_out.at[(1 - off) // 2], panel_in, off).start())

    def turn_edges(target, first, j):
        for b in range(blocks):
            span = slice(b * rows, (b + 1) * rows)
            target[span, first:first + rows] = wide[j * rows:(j + 1) * rows, span].T

    deep = width // CHUNKS

    def turn_x(i):
        for b in range(blocks):
            span = slice(b * rows, (b + 1) * rows)
            x_t[i, :, span] = x[span, i * deep:(i + 1) * deep].T

    sources_copy.wait()
    mweight_copy.wait()
    first = mweight[0].astype(F32)
    second = mweight[1].astype(F32)
    for j in range(3):
        hit = [jnp.where(sources[0, k] - me + 1 == j, 1.0, 0.0).astype(F32) for k in range(2)]
        mixed = (first * hit[0] + second * hit[1]).astype(BF16)
        near[j] = mixed
        near_t[j] = mixed.T
    turn_edges(wide_own_t, 0, 1)
    turn_x(0)
    mesh_copy.wait()
    agg_copy.wait()

    partial = [0.0] * HALVES
    for h in range(HALVES):
        received(0, h, panel_in)
        landed = panels[rows:2 * rows, cols[h]]
        for slot in range(2):
            landed = landed + panel_in[slot, :, cols[h]].astype(F32)
        landed = landed.astype(BF16)
        for n in range(HALVES):
            partial[n] = partial[n] + dot(landed, agg_w[cols[h], cols[n]])
            if h == HALVES - 1:
                pre = partial[n]
                sig = sigmoid(pre)
                upd[:, cols[n]] = (mesh[:, cols[n]].astype(F32) + pre * sig).astype(BF16)
                both(lambda off: halo(1, n, upd, upd_in, off).start())
                mesh_slope[:, cols[n]] = sig * (1.0 + pre * (1.0 - sig))

    own = dot(near[1], upd[...])

    turn_edges(wide_side_t, 0, 0)
    turn_edges(wide_side_t, rows, 2)
    proc_copy.wait()
    cot_copy.wait()

    proc_pre = 0.0
    for h in range(HALVES):
        received(1, h, upd_in)
        mixed = own[:, cols[h]] + dot(near[0], upd_in[0, :, cols[h]]) + dot(near[2], upd_in[1, :, cols[h]])
        proc_pre = proc_pre + dot(mixed.astype(BF16), proc_w[cols[h], :])
    proc_sig = sigmoid(proc_pre)
    proc_slope = proc_sig * (1.0 + proc_pre * (1.0 - proc_sig))
    upstream = cot[...].astype(F32)
    proc_delta = (upstream * proc_slope).astype(BF16)
    backs = []
    for n in range(HALVES):
        back = dot_t(proc_delta, proc_w[cols[n], :]).astype(BF16)
        for off in (far, -far):
            push_out[(1 - off) // 2, :, cols[n]] = dot(near_t[1 + off], back).astype(BF16)
        both(lambda off: halo(2, n, push_out.at[(1 - off) // 2], push_in, off).start())
        backs.append(back)
    for n in range(HALVES):
        mesh_grad[:, cols[n]] = upstream[:, cols[n]] + dot(near_t[1], backs[n])
    result[...] = (upd[...].astype(F32) + proc_pre * proc_sig).astype(BF16)
    result_copy = local(result, result_h.at[0], out_sem.at[CHUNKS])
    turn_x(1)
    turn_x(2)

    partial = [0.0] * HALVES
    for h in range(HALVES):
        received(2, h, push_in)
        landed = mesh_grad[:, cols[h]]
        for slot in range(2):
            landed = landed + push_in[slot, :, cols[h]].astype(F32)
        landed = (landed * mesh_slope[:, cols[h]]).astype(BF16)
        for n in range(HALVES):
            partial[n] = partial[n] + dot_t(landed, agg_w[cols[n], cols[h]])
            if h == HALVES - 1:
                agg[:, cols[n]] = partial[n].astype(BF16)
                both(lambda off: halo(3, n, agg, agg_in, off).start())

    for i in range(CHUNKS):
        span = pl.ds(i * step, step)
        own_grad[span] = dot(wide_own_t[span], agg[...])
    turn_x(3)

    for h in range(HALVES):
        received(3, h, agg_in)
        sides = agg_in[:, :, cols[h]].reshape(2 * rows, half)
        for i in range(CHUNKS):
            span = pl.ds(i * step, step)
            grad = own_grad[span, cols[h]] + dot(wide_side_t[span], sides)
            enc_delta[span, cols[h]] = (grad * slopes[span, cols[h]]).astype(BF16)

    def grid_part(i):
        span = pl.ds(i * step, step)
        grid_out[span] = dot_t(enc_delta[span], enc_w[...]).astype(BF16)
        return local(grid_out.at[span], grid_h.at[0, span], out_sem.at[i])

    if not fused:
        for i in range(CHUNKS):
            part[i] = dot(x_t[i], enc_delta[...]) * scale
        final_copy = local(part, final_h, out_sem.at[CHUNKS + 1])
        grid_copies = [grid_part(i) for i in range(CHUNKS)]
    else:
        share = part.shape[2]
        mine = share // members

        def pair(z):
            return pltpu.make_async_remote_copy(
                src_ref=part_out.at[z, 1 - core], dst_ref=pair_in.at[z],
                send_sem=a_send.at[z], recv_sem=a_recv.at[z],
                device_id={"grid": me + 1 - 2 * core}, device_id_type=MESH)

        def across(z, d, arriving):
            peer = lax.rem(ens + d, members)
            slot = peer if arriving else ens
            return pltpu.make_async_remote_copy(
                src_ref=quarter_out.at[z, peer], dst_ref=ens_in.at[z, slot],
                send_sem=b_send.at[z, peer], recv_sem=b_recv.at[z, slot],
                device_id={"ens": peer}, device_id_type=MESH)

        def along(d, arriving):
            peer = lax.rem(level + d, levels)
            slot = peer if arriving else level
            return pltpu.make_async_remote_copy(
                src_ref=summed_out.at[peer], dst_ref=z_in.at[slot],
                send_sem=c_send.at[peer], recv_sem=c_recv.at[slot],
                device_id={"grid": peer * 2 + core}, device_id_type=MESH)

        def gather(d, arriving):
            peer = lax.rem(ens + d, members)
            slot = peer if arriving else ens
            return pltpu.make_async_remote_copy(
                src_ref=final.at[ens], dst_ref=final.at[slot],
                send_sem=d_send.at[peer], recv_sem=d_recv.at[slot],
                device_id={"ens": peer}, device_id_type=MESH)

        order = [lax.rem(level + d, levels) for d in list(range(1, levels)) + [0]]
        def weigh(z):
            value = (dot(x_t[z], enc_delta[...]) * scale).reshape(2, share, width)
            part[z] = value
            part_out[z] = value.astype(BF16)
            pair(z).start()

        def pair_up(z):
            pair(z).wait_recv()
            value = part[z, core] + pair_in[z].astype(F32)
            value = value.reshape(members, mine, width)
            quarter[z] = value
            quarter_out[z] = value.astype(BF16)
            for d in range(1, members):
                across(z, d, False).start()

        def add_up(z):
            value = quarter[z, ens]
            for d in range(1, members):
                across(z, d, True).wait_recv()
                value = value + ens_in[z, lax.rem(ens + d, members)].astype(F32)
            return value

        weigh(order[0])
        for n in range(1, levels):
            weigh(order[n])
            pair_up(order[n - 1])
        grid_copies = [grid_part(0)]
        pair_up(order[-1])
        grid_copies.append(grid_part(1))
        for n in range(levels - 1):
            summed_out[order[n]] = add_up(order[n]).astype(BF16)
            along(n + 1, False).start()
            if n + 2 < CHUNKS:
                grid_copies.append(grid_part(n + 2))
        summed[...] = add_up(level)
        value = summed[...]
        for d in range(1, levels):
            along(d, True).wait_recv()
            value = value + z_in[lax.rem(level + d, levels)].astype(F32)
        final[ens] = value.astype(BF16)
        for d in range(1, members):
            gather(d, False).start()
        for d in range(1, members):
            gather(d, True).wait_recv()
        final_out[...] = final[...].astype(F32)
        final_copy = local(final_out, final_h, out_sem.at[CHUNKS + 1])
        for z in order:
            pair(z).wait_send()
            for d in range(1, members):
                across(z, d, False).wait_send()
        for d in range(1, levels):
            along(d, False).wait_send()
        for d in range(1, members):
            gather(d, False).wait_send()

    for turn, landing in enumerate((panel_in, upd_in, push_in, agg_in)):
        for h in range(HALVES):
            sent(turn, h, landing)
    result_copy.wait()
    for copy in grid_copies:
        copy.wait()
    final_copy.wait()


def leave(result, grid_grad, grad, result_out, grid_out, grad_out, one, two, three, in_sem, out_sem):
    step = grid_grad.shape[1] // CHUNKS
    moves = [(result, one, result_out), (grad, three, grad_out)]
    for i in range(CHUNKS):
        span = pl.ds(i * step, step)
        moves.append((grid_grad.at[:, span], two.at[:, span], grid_out.at[:, span]))
    arriving = [pltpu.make_async_copy(a, b, in_sem.at[i]) for i, (a, b, c) in enumerate(moves)]
    leaving = [pltpu.make_async_copy(b, c, out_sem.at[i]) for i, (a, b, c) in enumerate(moves)]
    for copy in arriving:
        copy.start()
    for first, second in zip(arriving, leaving):
        first.wait()
        second.start()
    for copy in leaving:
        copy.wait()


def on_device(
    bands, members,
    grid_latent, mesh_latent, cotangent, edge_weights, edge_targets, mesh_weights, mesh_sources,
    encode_weight, aggregate_weight, process_weight,
):
    unused, total, width = grid_latent.shape
    rows = mesh_latent.shape[1]
    share = width // bands
    levels = max(bands // 2, 1)
    fused = bands % 2 == 0 and levels == CHUNKS and share % (16 * members) == 0
    scale = 1.0 / float(members * total * bands) ** 0.5
    mine = share // members if fused else 16
    gshape = (CHUNKS, 2, width // CHUNKS // 2, width) if fused else (CHUNKS, width // CHUNKS, width)
    last = (members, mine, width) if fused else gshape
    vm = pltpu.VMEM
    dma = pltpu.SemaphoreType.DMA
    panel = (2, rows, width)
    quarters = (CHUNKS, members, mine, width)
    scratch = [
        vm((total, width), BF16), vm((rows, width), BF16), vm((rows, width), BF16),
        vm(edge_weights.shape, BF16),
        pltpu.SMEM(edge_targets.shape[::-1], jnp.int32), vm(mesh_weights.shape[1:], BF16),
        pltpu.SMEM(mesh_sources.shape, jnp.int32),
        vm((width, width), BF16), vm((width, width), BF16), vm((width, width), BF16),
        vm((3 * rows, total), BF16), vm((total, rows), BF16), vm((total, 2 * rows), BF16),
        vm((3, rows, rows), BF16), vm((3, rows, rows), BF16), vm((CHUNKS, width // CHUNKS, total), BF16),
        vm((total, width), F32), vm((3 * rows, width), F32),
        vm(panel, BF16), vm(panel, BF16), vm((rows, width), BF16), vm(panel, BF16),
        vm(panel, BF16), vm(panel, BF16), vm((rows, width), BF16), vm(panel, BF16),
        vm((rows, width), F32), vm((rows, width), F32),
        vm((total, width), F32), vm((total, width), BF16), vm((total, width), BF16), vm((rows, width), BF16),
        vm(gshape, F32), vm(gshape, BF16), vm((CHUNKS, width // CHUNKS // 2, width), BF16),
        vm(quarters, F32), vm(quarters, BF16), vm(quarters, BF16),
        vm((mine, width), F32), vm((CHUNKS, mine, width), BF16), vm((CHUNKS, mine, width), BF16),
        vm((members, mine, width), BF16), vm((members, mine, width), F32),
        dma((9 + CHUNKS,)), dma((CHUNKS + 2,)), dma((4, 2, HALVES)), dma((4, 2, HALVES)),
        dma((CHUNKS,)), dma((CHUNKS,)), dma((CHUNKS, members)), dma((CHUNKS, members)),
        dma((CHUNKS,)), dma((CHUNKS,)), dma((members,)), dma((members,)),
    ]
    hbm = pl.BlockSpec(memory_space=pltpu.HBM)
    anywhere = pl.BlockSpec(memory_space=pl.ANY)
    result, grid_grad, grad = pl.pallas_call(
        functools.partial(kernel, bands, members, scale, fused),
        out_shape=(
            jax.ShapeDtypeStruct(mesh_latent.shape, BF16),
            jax.ShapeDtypeStruct(grid_latent.shape, BF16),
            jax.ShapeDtypeStruct(last, F32),
        ),
        in_specs=[hbm] * 10,
        out_specs=(anywhere,) * 3,
        scratch_shapes=scratch,
        compiler_params=pltpu.CompilerParams(
            collective_id=0, has_side_effects=True, vmem_limit_bytes=63 * 1024 * 1024
        ),
    )(
        grid_latent, mesh_latent, cotangent, edge_weights, edge_targets.T, mesh_weights, mesh_sources,
        encode_weight, aggregate_weight, process_weight,
    )
    if fused:
        result, grid_grad, grad = pl.pallas_call(
            leave,
            out_shape=tuple(jax.ShapeDtypeStruct(a.shape, a.dtype) for a in (result, grid_grad, grad)),
            in_specs=[anywhere] * 3,
            out_specs=(hbm,) * 3,
            scratch_shapes=[vm(a.shape, a.dtype) for a in (result, grid_grad, grad)] + [dma((2 + CHUNKS,))] * 2,
            compiler_params=pltpu.CompilerParams(vmem_limit_bytes=63 * 1024 * 1024),
        )(result, grid_grad, grad)
        grad = grad.reshape(share, width)
    else:
        summed = lax.psum(grad.reshape(width, width), ("ens", "grid"))
        grad = lax.dynamic_slice_in_dim(summed, lax.axis_index("grid") * share, share, 0)
    return result, grid_grad, grad


def solution(mesh):
    return jax.shard_map(
        functools.partial(on_device, mesh.shape["grid"], mesh.shape["ens"]),
        mesh=mesh,
        in_specs=(
            P("ens", "grid", None),
            P("ens", "grid", None),
            P("ens", "grid", None),
            P("grid", None, None, None),
            P("grid", None),
            P("grid", None, None, None),
            P("grid", None),
            P(),
            P(),
            P(),
        ),
        out_specs=(P("ens", "grid", None), P("ens", "grid", None), P("grid", None)),
        check_vma=False,
    )
```

```python
import functools

import jax
import jax.numpy as jnp
from jax import lax
from jax.experimental import pallas as pl
from jax.experimental.pallas import tpu as pltpu
from jax.sharding import PartitionSpec as P

MESH = pl.DeviceIdType.MESH
F32 = jnp.float32
BF16 = jnp.bfloat16
CHUNKS = 4
HALVES = 2


def sigmoid(value):
    return 0.5 + 0.5 * jnp.tanh(0.5 * value)


def dot(a, b):
    return jnp.dot(a, b, preferred_element_type=F32)


def dot_t(a, b):
    return lax.dot_general(a, b, (((1,), (1,)), ((), ())), preferred_element_type=F32)


def kernel(
    bands, members, scale, fused,
    x_h, mesh_h, cot_h, edge_h, targets_h, mweight_h, sources_h, enc_w_h, agg_w_h, proc_w_h,
    result_h, grid_h, final_h,
    x, mesh, cot, edge, targets, mweight, sources, enc_w, agg_w, proc_w,
    wide, wide_own_t, wide_side_t, near, near_t, x_t,
    slopes, panels, panel_out, panel_in, upd, upd_in, push_out, push_in, agg, agg_in,
    mesh_slope, mesh_grad, own_grad, enc_delta, grid_out, result,
    part, part_out, pair_in, quarter, quarter_out, ens_in, summed, summed_out, z_in, final, final_out,
    in_sem, out_sem, halo_send, halo_recv, a_send, a_recv, b_send, b_recv, c_send, c_recv, d_send, d_recv,
):
    me = lax.axis_index("grid")
    ens = lax.axis_index("ens")
    core = lax.rem(me, 2)
    level = me // 2
    levels = bands // 2
    rows = mesh.shape[0]
    total = x.shape[0]
    blocks = total // rows
    step = total // CHUNKS
    width = x.shape[1]
    far = 2 * core - 1
    far_there = (me + far >= 0) & (me + far < bands)

    def both(act):
        pl.when(far_there)(lambda: act(far))
        act(-far)

    def local(src, dst, sem):
        copy = pltpu.make_async_copy(src, dst, sem)
        copy.start()
        return copy

    targets_copy = local(targets_h, targets, in_sem.at[7])
    edge_copy = local(edge_h, edge, in_sem.at[0])
    enc_copy = local(enc_w_h, enc_w, in_sem.at[1])
    x_copies = [
        local(x_h.at[0, pl.ds(i * step, step)], x.at[pl.ds(i * step, step)], in_sem.at[8 + i])
        for i in range(CHUNKS)
    ]
    agg_copy = local(agg_w_h, agg_w, in_sem.at[2])
    mesh_copy = local(mesh_h.at[0], mesh, in_sem.at[3])
    mweight_copy = local(mweight_h.at[0], mweight, in_sem.at[4])
    proc_copy = local(proc_w_h, proc_w, in_sem.at[5])
    cot_copy = local(cot_h.at[0], cot, in_sem.at[6])
    sources_copy = local(sources_h, sources, in_sem.at[8 + CHUNKS])

    barrier = pltpu.get_barrier_semaphore()

    def greet(**where):
        pl.semaphore_signal(barrier, inc=1, device_id=where, device_id_type=MESH)

    both(lambda off: greet(grid=me + off))
    expected = 1 + far_there.astype(jnp.int32)
    if fused:
        for d in range(1, members):
            greet(ens=lax.rem(ens + d, members))
        for d in range(1, levels):
            greet(grid=lax.rem(level + d, levels) * 2 + core)
        expected = expected + (members - 1) + (levels - 1)

    @pl.when(jnp.logical_not(far_there))
    def clear():
        slot = (1 + far) // 2
        for ref in (panel_in, upd_in, push_in, agg_in):
            ref[slot] = jnp.zeros(ref.shape[1:], ref.dtype)

    targets_copy.wait()
    edge_copy.wait()
    for b in range(blocks):
        first = edge[b, 0].astype(F32)
        second = edge[b, 1].astype(F32)
        for j in range(3):
            hit = [jnp.where(targets[k, b] - me + 1 == j, 1.0, 0.0).astype(F32) for k in range(2)]
            wide[j * rows:(j + 1) * rows, b * rows:(b + 1) * rows] = (first * hit[0] + second * hit[1]).astype(BF16)

    half = width // HALVES
    cols = [slice(h * half, (h + 1) * half) for h in range(HALVES)]

    def halo(turn, h, source, landing, off):
        slot = (1 - off) // 2
        return pltpu.make_async_remote_copy(
            src_ref=source.at[:, cols[h]],
            dst_ref=landing.at[slot, :, cols[h]],
            send_sem=halo_send.at[turn, slot, h],
            recv_sem=halo_recv.at[turn, slot, h],
            device_id={"grid": me + off},
            device_id_type=MESH,
        )

    def received(turn, h, landing):
        act = lambda off: halo(turn, h, landing.at[(1 - off) // 2], landing, off).wait_recv()
        act(far)
        pl.when(far_there)(lambda: act(-far))

    def sent(turn, h, landing):
        both(lambda off: halo(turn, h, landing.at[(1 - off) // 2], landing, off).wait_send())

    enc_copy.wait()
    for h in range(HALVES):
        for i in range(CHUNKS):
            if h == 0:
                x_copies[i].wait()
            span = pl.ds(i * step, step)
            value = dot(x[span], enc_w[:, cols[h]])
            sig = sigmoid(value)
            message = value * sig
            slopes[span, cols[h]] = sig + message * (1.0 - sig)
            term = dot(wide[:, i * step:(i + 1) * step], message.astype(BF16))
            panels[:, cols[h]] = term if i == 0 else panels[:, cols[h]] + term
        if h == 0:
            pl.semaphore_wait(barrier, expected)
        for off in (far, -far):
            panel_out[(1 - off) // 2, :, cols[h]] = panels[pl.ds((1 + off) * rows, rows), cols[h]].astype(BF16)
        both(lambda off: halo(0, h, panel_out.at[(1 - off) // 2], panel_in, off).start())

    def turn_edges(target, first, j):
        for b in range(blocks):
            span = slice(b * rows, (b + 1) * rows)
            target[span, first:first + rows] = wide[j * rows:(j + 1) * rows, span].T

    deep = width // CHUNKS

    def turn_x(i):
        for b in range(blocks):
            span = slice(b * rows, (b + 1) * rows)
            x_t[i * deep:(i + 1) * deep, span] = x[span, i * deep:(i + 1) * deep].T

    sources_copy.wait()
    mweight_copy.wait()
    first = mweight[0].astype(F32)
    second = mweight[1].astype(F32)
    for j in range(3):
        hit = [jnp.where(sources[0, k] - me + 1 == j, 1.0, 0.0).astype(F32) for k in range(2)]
        mixed = (first * hit[0] + second * hit[1]).astype(BF16)
        near[j] = mixed
        near_t[j] = mixed.T
    turn_edges(wide_own_t, 0, 1)
    turn_x(0)
    mesh_copy.wait()
    agg_copy.wait()

    partial = [0.0] * HALVES
    for h in range(HALVES):
        received(0, h, panel_in)
        landed = panels[rows:2 * rows, cols[h]]
        for slot in range(2):
            landed = landed + panel_in[slot, :, cols[h]].astype(F32)
        landed = landed.astype(BF16)
        for n in range(HALVES):
            partial[n] = partial[n] + dot(landed, agg_w[cols[h], cols[n]])
            if h == HALVES - 1:
                pre = partial[n]
                sig = sigmoid(pre)
                upd[:, cols[n]] = (mesh[:, cols[n]].astype(F32) + pre * sig).astype(BF16)
                both(lambda off: halo(1, n, upd, upd_in, off).start())
                mesh_slope[:, cols[n]] = sig * (1.0 + pre * (1.0 - sig))

    own = dot(near[1], upd[...])

    turn_edges(wide_side_t, 0, 0)
    turn_edges(wide_side_t, rows, 2)
    proc_copy.wait()
    cot_copy.wait()

    proc_pre = 0.0
    for h in range(HALVES):
        received(1, h, upd_in)
        mixed = own[:, cols[h]] + dot(near[0], upd_in[0, :, cols[h]]) + dot(near[2], upd_in[1, :, cols[h]])
        proc_pre = proc_pre + dot(mixed.astype(BF16), proc_w[cols[h], :])
    proc_sig = sigmoid(proc_pre)
    proc_slope = proc_sig * (1.0 + proc_pre * (1.0 - proc_sig))
    upstream = cot[...].astype(F32)
    proc_delta = (upstream * proc_slope).astype(BF16)
    backs = []
    for n in range(HALVES):
        back = dot_t(proc_delta, proc_w[cols[n], :]).astype(BF16)
        for off in (far, -far):
            push_out[(1 - off) // 2, :, cols[n]] = dot(near_t[1 + off], back).astype(BF16)
        both(lambda off: halo(2, n, push_out.at[(1 - off) // 2], push_in, off).start())
        backs.append(back)
    for n in range(HALVES):
        mesh_grad[:, cols[n]] = upstream[:, cols[n]] + dot(near_t[1], backs[n])
    result[...] = (upd[...].astype(F32) + proc_pre * proc_sig).astype(BF16)
    result_copy = local(result, result_h.at[0], out_sem.at[CHUNKS])
    turn_x(1)
    turn_x(2)

    partial = [0.0] * HALVES
    for h in range(HALVES):
        received(2, h, push_in)
        landed = mesh_grad[:, cols[h]]
        for slot in range(2):
            landed = landed + push_in[slot, :, cols[h]].astype(F32)
        landed = (landed * mesh_slope[:, cols[h]]).astype(BF16)
        for n in range(HALVES):
            partial[n] = partial[n] + dot_t(landed, agg_w[cols[n], cols[h]])
            if h == HALVES - 1:
                agg[:, cols[n]] = partial[n].astype(BF16)
                both(lambda off: halo(3, n, agg, agg_in, off).start())

    for i in range(CHUNKS):
        span = pl.ds(i * step, step)
        own_grad[span] = dot(wide_own_t[span], agg[...])
    turn_x(3)

    def deltas(h):
        received(3, h, agg_in)
        sides = agg_in[:, :, cols[h]].reshape(2 * rows, half)
        for i in range(CHUNKS):
            span = pl.ds(i * step, step)
            grad = own_grad[span, cols[h]] + dot(wide_side_t[span], sides)
            enc_delta[span, cols[h]] = (grad * slopes[span, cols[h]]).astype(BF16)

    def grid_part(i):
        span = pl.ds(i * step, step)
        grid_out[span] = dot_t(enc_delta[span], enc_w[...]).astype(BF16)
        return local(grid_out.at[span], grid_h.at[0, span], out_sem.at[i])

    if not fused:
        for h in range(HALVES):
            deltas(h)
            part[:, cols[h]] = dot(x_t[...], enc_delta[:, cols[h]]) * scale
        final_copy = local(part, final_h, out_sem.at[CHUNKS + 1])
        grid_copies = [grid_part(i) for i in range(CHUNKS)]
    else:
        share = part.shape[3]
        mine = share // members

        def pair(h):
            return pltpu.make_async_remote_copy(
                src_ref=part_out.at[h, 1 - core], dst_ref=pair_in.at[h],
                send_sem=a_send.at[h], recv_sem=a_recv.at[h],
                device_id={"grid": me + 1 - 2 * core}, device_id_type=MESH)

        def across(h, d, arriving):
            peer = lax.rem(ens + d, members)
            slot = peer if arriving else ens
            return pltpu.make_async_remote_copy(
                src_ref=quarter_out.at[h, peer], dst_ref=ens_in.at[h, slot],
                send_sem=b_send.at[h, peer], recv_sem=b_recv.at[h, slot],
                device_id={"ens": peer}, device_id_type=MESH)

        def along(h, d, arriving):
            peer = lax.rem(level + d, levels)
            slot = peer if arriving else level
            return pltpu.make_async_remote_copy(
                src_ref=summed_out.at[h, peer], dst_ref=z_in.at[h, slot],
                send_sem=c_send.at[h, peer], recv_sem=c_recv.at[h, slot],
                device_id={"grid": peer * 2 + core}, device_id_type=MESH)

        def gather(h, d, arriving):
            peer = lax.rem(ens + d, members)
            slot = peer if arriving else ens
            return pltpu.make_async_remote_copy(
                src_ref=final.at[h, ens], dst_ref=final.at[h, slot],
                send_sem=d_send.at[h, peer], recv_sem=d_recv.at[h, slot],
                device_id={"ens": peer}, device_id_type=MESH)

        def weigh(h):
            value = (dot(x_t[...], enc_delta[:, cols[h]]) * scale).reshape(levels, 2, share, half)
            for c in range(2):
                part[h, c] = value[:, c]
                part_out[h, c] = value[:, c].astype(BF16)
            pair(h).start()

        def pair_up(h):
            pair(h).wait_recv()
            value = part[h, core] + pair_in[h].astype(F32)
            for q in range(members):
                block = value[:, q * mine:(q + 1) * mine]
                quarter[h, q] = block
                quarter_out[h, q] = block.astype(BF16)
            for d in range(1, members):
                across(h, d, False).start()

        def add_up(h):
            value = quarter[h, ens]
            for d in range(1, members):
                across(h, d, True).wait_recv()
                value = value + ens_in[h, lax.rem(ens + d, members)].astype(F32)
            summed[h] = value
            summed_out[h] = value.astype(BF16)
            for d in range(1, levels):
                along(h, d, False).start()

        def finish(h):
            value = summed[h, level]
            for d in range(1, levels):
                along(h, d, True).wait_recv()
                value = value + z_in[h, lax.rem(level + d, levels)].astype(F32)
            final[h, ens] = value.astype(BF16)
            for d in range(1, members):
                gather(h, d, False).start()

        deltas(0)
        weigh(0)
        deltas(1)
        pair_up(0)
        weigh(1)
        grid_copies = [grid_part(0)]
        pair_up(1)
        grid_copies += [grid_part(1), grid_part(2)]
        add_up(0)
        grid_copies.append(grid_part(3))
        add_up(1)
        for h in range(HALVES):
            finish(h)
        for h in range(HALVES):
            for d in range(1, members):
                gather(h, d, True).wait_recv()
        for h in range(HALVES):
            final_out[:, :, cols[h]] = final[h].astype(F32)
        final_copy = local(final_out, final_h, out_sem.at[CHUNKS + 1])
        for h in range(HALVES):
            pair(h).wait_send()
            for d in range(1, members):
                across(h, d, False).wait_send()
                gather(h, d, False).wait_send()
            for d in range(1, levels):
                along(h, d, False).wait_send()

    for turn, landing in enumerate((panel_in, upd_in, push_in, agg_in)):
        for h in range(HALVES):
            sent(turn, h, landing)
    result_copy.wait()
    for copy in grid_copies:
        copy.wait()
    final_copy.wait()


def leave(result, grid_grad, grad, result_out, grid_out, grad_out, one, two, three, in_sem, out_sem):
    step = grid_grad.shape[1] // CHUNKS
    moves = [(result, one, result_out), (grad, three, grad_out)]
    for i in range(CHUNKS):
        span = pl.ds(i * step, step)
        moves.append((grid_grad.at[:, span], two.at[:, span], grid_out.at[:, span]))
    arriving = [pltpu.make_async_copy(a, b, in_sem.at[i]) for i, (a, b, c) in enumerate(moves)]
    leaving = [pltpu.make_async_copy(b, c, out_sem.at[i]) for i, (a, b, c) in enumerate(moves)]
    for copy in arriving:
        copy.start()
    for first, second in zip(arriving, leaving):
        first.wait()
        second.start()
    for copy in leaving:
        copy.wait()


def on_device(
    bands, members,
    grid_latent, mesh_latent, cotangent, edge_weights, edge_targets, mesh_weights, mesh_sources,
    encode_weight, aggregate_weight, process_weight,
):
    unused, total, width = grid_latent.shape
    rows = mesh_latent.shape[1]
    share = width // bands
    levels = max(bands // 2, 1)
    fused = bands % 2 == 0 and levels == CHUNKS and share % (16 * members) == 0
    scale = 1.0 / float(members * total * bands) ** 0.5
    mine = share // members if fused else 16
    half = width // HALVES
    gshape = (HALVES, 2, CHUNKS, width // CHUNKS // 2, half) if fused else (width, width)
    last = (members, mine, width) if fused else gshape
    vm = pltpu.VMEM
    dma = pltpu.SemaphoreType.DMA
    panel = (2, rows, width)
    quarters = (HALVES, members, CHUNKS, mine, half)
    levelled = (HALVES, CHUNKS, mine, half)
    scratch = [
        vm((total, width), BF16), vm((rows, width), BF16), vm((rows, width), BF16),
        vm(edge_weights.shape, BF16),
        pltpu.SMEM(edge_targets.shape[::-1], jnp.int32), vm(mesh_weights.shape[1:], BF16),
        pltpu.SMEM(mesh_sources.shape, jnp.int32),
        vm((width, width), BF16), vm((width, width), BF16), vm((width, width), BF16),
        vm((3 * rows, total), BF16), vm((total, rows), BF16), vm((total, 2 * rows), BF16),
        vm((3, rows, rows), BF16), vm((3, rows, rows), BF16), vm((width, total), BF16),
        vm((total, width), F32), vm((3 * rows, width), F32),
        vm(panel, BF16), vm(panel, BF16), vm((rows, width), BF16), vm(panel, BF16),
        vm(panel, BF16), vm(panel, BF16), vm((rows, width), BF16), vm(panel, BF16),
        vm((rows, width), F32), vm((rows, width), F32),
        vm((total, width), F32), vm((total, width), BF16), vm((total, width), BF16), vm((rows, width), BF16),
        vm(gshape, F32), vm(gshape, BF16), vm((HALVES, CHUNKS, width // CHUNKS // 2, half), BF16),
        vm(quarters, F32), vm(quarters, BF16), vm(quarters, BF16),
        vm(levelled, F32), vm(levelled, BF16), vm(levelled, BF16),
        vm((HALVES, members, mine, half), BF16), vm((members, mine, width), F32),
        dma((9 + CHUNKS,)), dma((CHUNKS + 2,)), dma((4, 2, HALVES)), dma((4, 2, HALVES)),
        dma((HALVES,)), dma((HALVES,)), dma((HALVES, members)), dma((HALVES, members)),
        dma((HALVES, CHUNKS)), dma((HALVES, CHUNKS)), dma((HALVES, members)), dma((HALVES, members)),
    ]
    hbm = pl.BlockSpec(memory_space=pltpu.HBM)
    anywhere = pl.BlockSpec(memory_space=pl.ANY)
    result, grid_grad, grad = pl.pallas_call(
        functools.partial(kernel, bands, members, scale, fused),
        out_shape=(
            jax.ShapeDtypeStruct(mesh_latent.shape, BF16),
            jax.ShapeDtypeStruct(grid_latent.shape, BF16),
            jax.ShapeDtypeStruct(last, F32),
        ),
        in_specs=[hbm] * 10,
        out_specs=(anywhere,) * 3,
        scratch_shapes=scratch,
        compiler_params=pltpu.CompilerParams(
            collective_id=0, has_side_effects=True, vmem_limit_bytes=63 * 1024 * 1024
        ),
    )(
        grid_latent, mesh_latent, cotangent, edge_weights, edge_targets.T, mesh_weights, mesh_sources,
        encode_weight, aggregate_weight, process_weight,
    )
    if fused:
        result, grid_grad, grad = pl.pallas_call(
            leave,
            out_shape=tuple(jax.ShapeDtypeStruct(a.shape, a.dtype) for a in (result, grid_grad, grad)),
            in_specs=[anywhere] * 3,
            out_specs=(hbm,) * 3,
            scratch_shapes=[vm(a.shape, a.dtype) for a in (result, grid_grad, grad)] + [dma((2 + CHUNKS,))] * 2,
            compiler_params=pltpu.CompilerParams(vmem_limit_bytes=63 * 1024 * 1024),
        )(result, grid_grad, grad)
        grad = grad.reshape(share, width)
    else:
        summed = lax.psum(grad.reshape(width, width), ("ens", "grid"))
        grad = lax.dynamic_slice_in_dim(summed, lax.axis_index("grid") * share, share, 0)
    return result, grid_grad, grad


def solution(mesh):
    return jax.shard_map(
        functools.partial(on_device, mesh.shape["grid"], mesh.shape["ens"]),
        mesh=mesh,
        in_specs=(
            P("ens", "grid", None),
            P("ens", "grid", None),
            P("ens", "grid", None),
            P("grid", None, None, None),
            P("grid", None),
            P("grid", None, None, None),
            P("grid", None),
            P(),
            P(),
            P(),
        ),
        out_specs=(P("ens", "grid", None), P("ens", "grid", None), P("grid", None)),
        check_vma=False,
    )
```

```python
import functools

import jax
import jax.numpy as jnp
from jax import lax
from jax.experimental import pallas as pl
from jax.experimental.pallas import tpu as pltpu
from jax.sharding import PartitionSpec as P

MESH = pl.DeviceIdType.MESH
F32 = jnp.float32
BF16 = jnp.bfloat16
CHUNKS = 4
HALVES = 2


def sigmoid(value):
    return 0.5 + 0.5 * jnp.tanh(0.5 * value)


def dot(a, b):
    return jnp.dot(a, b, preferred_element_type=F32)


def dot_t(a, b):
    return lax.dot_general(a, b, (((1,), (1,)), ((), ())), preferred_element_type=F32)


def kernel(
    bands, members, scale, fused,
    x_h, mesh_h, cot_h, edge_h, targets_h, mweight_h, sources_h, enc_w_h, agg_w_h, proc_w_h,
    result_h, grid_h, final_h,
    x, mesh, cot, edge, targets, mweight, sources, enc_w, agg_w, proc_w,
    wide, wide_own_t, wide_side_t, near, near_t, x_t,
    slopes, panels, panel_out, panel_in, upd, upd_in, push_out, push_in, agg, agg_in,
    mesh_slope, mesh_grad, own_grad, enc_delta, grid_out, result,
    part, part_out, pair_in, quarter, quarter_out, ens_in, summed, summed_out, z_in, final, final_out,
    in_sem, out_sem, halo_send, halo_recv, a_send, a_recv, b_send, b_recv, c_send, c_recv, d_send, d_recv,
):
    me = lax.axis_index("grid")
    ens = lax.axis_index("ens")
    core = lax.rem(me, 2)
    level = me // 2
    levels = bands // 2
    rows = mesh.shape[0]
    total = x.shape[0]
    blocks = total // rows
    step = total // CHUNKS
    width = x.shape[1]
    far = 2 * core - 1
    far_there = (me + far >= 0) & (me + far < bands)

    def both(act):
        pl.when(far_there)(lambda: act(far))
        act(-far)

    def local(src, dst, sem):
        copy = pltpu.make_async_copy(src, dst, sem)
        copy.start()
        return copy

    targets_copy = local(targets_h, targets, in_sem.at[7])
    edge_copy = local(edge_h, edge, in_sem.at[0])
    enc_copy = local(enc_w_h, enc_w, in_sem.at[1])
    x_copies = [
        local(x_h.at[0, pl.ds(i * step, step)], x.at[pl.ds(i * step, step)], in_sem.at[8 + i])
        for i in range(CHUNKS)
    ]
    agg_copy = local(agg_w_h, agg_w, in_sem.at[2])
    mesh_copy = local(mesh_h.at[0], mesh, in_sem.at[3])
    mweight_copy = local(mweight_h.at[0], mweight, in_sem.at[4])
    proc_copy = local(proc_w_h, proc_w, in_sem.at[5])
    cot_copy = local(cot_h.at[0], cot, in_sem.at[6])
    sources_copy = local(sources_h, sources, in_sem.at[8 + CHUNKS])

    barrier = pltpu.get_barrier_semaphore()

    def greet(**where):
        pl.semaphore_signal(barrier, inc=1, device_id=where, device_id_type=MESH)

    both(lambda off: greet(grid=me + off))
    expected = 1 + far_there.astype(jnp.int32)
    if fused:
        for d in range(1, members):
            greet(ens=lax.rem(ens + d, members))
        for d in range(1, levels):
            greet(grid=lax.rem(level + d, levels) * 2 + core)
        expected = expected + (members - 1) + (levels - 1)

    @pl.when(jnp.logical_not(far_there))
    def clear():
        slot = (1 + far) // 2
        for ref in (panel_in, upd_in, push_in, agg_in):
            ref[slot] = jnp.zeros(ref.shape[1:], ref.dtype)

    targets_copy.wait()
    edge_copy.wait()
    for b in range(blocks):
        first = edge[b, 0].astype(F32)
        second = edge[b, 1].astype(F32)
        for j in range(3):
            hit = [jnp.where(targets[k, b] - me + 1 == j, 1.0, 0.0).astype(F32) for k in range(2)]
            wide[j * rows:(j + 1) * rows, b * rows:(b + 1) * rows] = (first * hit[0] + second * hit[1]).astype(BF16)

    half = width // HALVES
    cols = [slice(h * half, (h + 1) * half) for h in range(HALVES)]

    def halo(turn, h, source, landing, off):
        slot = (1 - off) // 2
        return pltpu.make_async_remote_copy(
            src_ref=source.at[:, cols[h]],
            dst_ref=landing.at[slot, :, cols[h]],
            send_sem=halo_send.at[turn, slot, h],
            recv_sem=halo_recv.at[turn, slot, h],
            device_id={"grid": me + off},
            device_id_type=MESH,
        )

    def received(turn, h, landing):
        act = lambda off: halo(turn, h, landing.at[(1 - off) // 2], landing, off).wait_recv()
        act(far)
        pl.when(far_there)(lambda: act(-far))

    def sent(turn, h, landing):
        both(lambda off: halo(turn, h, landing.at[(1 - off) // 2], landing, off).wait_send())

    enc_copy.wait()
    for h in range(HALVES):
        for i in range(CHUNKS):
            if h == 0:
                x_copies[i].wait()
            span = pl.ds(i * step, step)
            value = dot(x[span], enc_w[:, cols[h]])
            sig = sigmoid(value)
            message = value * sig
            slopes[span, cols[h]] = sig + message * (1.0 - sig)
            term = dot(wide[:, i * step:(i + 1) * step], message.astype(BF16))
            panels[:, cols[h]] = term if i == 0 else panels[:, cols[h]] + term
        if h == 0:
            pl.semaphore_wait(barrier, expected)
        for off in (far, -far):
            panel_out[(1 - off) // 2, :, cols[h]] = panels[pl.ds((1 + off) * rows, rows), cols[h]].astype(BF16)
        both(lambda off: halo(0, h, panel_out.at[(1 - off) // 2], panel_in, off).start())

    def turn_edges(target, first, j):
        for b in range(blocks):
            span = slice(b * rows, (b + 1) * rows)
            target[span, first:first + rows] = wide[j * rows:(j + 1) * rows, span].T

    deep = width // CHUNKS

    def turn_x(i):
        for b in range(blocks):
            span = slice(b * rows, (b + 1) * rows)
            x_t[i, :, span] = x[span, i * deep:(i + 1) * deep].T

    sources_copy.wait()
    mweight_copy.wait()
    first = mweight[0].astype(F32)
    second = mweight[1].astype(F32)
    for j in range(3):
        hit = [jnp.where(sources[0, k] - me + 1 == j, 1.0, 0.0).astype(F32) for k in range(2)]
        mixed = (first * hit[0] + second * hit[1]).astype(BF16)
        near[j] = mixed
        near_t[j] = mixed.T
    turn_edges(wide_own_t, 0, 1)
    turn_x(0)
    mesh_copy.wait()
    agg_copy.wait()

    partial = [0.0] * HALVES
    for h in range(HALVES):
        received(0, h, panel_in)
        landed = panels[rows:2 * rows, cols[h]]
        for slot in range(2):
            landed = landed + panel_in[slot, :, cols[h]].astype(F32)
        landed = landed.astype(BF16)
        for n in range(HALVES):
            partial[n] = partial[n] + dot(landed, agg_w[cols[h], cols[n]])
            if h == HALVES - 1:
                pre = partial[n]
                sig = sigmoid(pre)
                upd[:, cols[n]] = (mesh[:, cols[n]].astype(F32) + pre * sig).astype(BF16)
                both(lambda off: halo(1, n, upd, upd_in, off).start())
                mesh_slope[:, cols[n]] = sig * (1.0 + pre * (1.0 - sig))

    own = dot(near[1], upd[...])

    turn_edges(wide_side_t, 0, 0)
    turn_edges(wide_side_t, rows, 2)
    proc_copy.wait()
    cot_copy.wait()

    proc_pre = 0.0
    for h in range(HALVES):
        received(1, h, upd_in)
        mixed = own[:, cols[h]] + dot(near[0], upd_in[0, :, cols[h]]) + dot(near[2], upd_in[1, :, cols[h]])
        proc_pre = proc_pre + dot(mixed.astype(BF16), proc_w[cols[h], :])
    proc_sig = sigmoid(proc_pre)
    proc_slope = proc_sig * (1.0 + proc_pre * (1.0 - proc_sig))
    upstream = cot[...].astype(F32)
    proc_delta = (upstream * proc_slope).astype(BF16)
    backs = []
    for n in range(HALVES):
        back = dot_t(proc_delta, proc_w[cols[n], :]).astype(BF16)
        for off in (far, -far):
            push_out[(1 - off) // 2, :, cols[n]] = dot(near_t[1 + off], back).astype(BF16)
        both(lambda off: halo(2, n, push_out.at[(1 - off) // 2], push_in, off).start())
        backs.append(back)
    for n in range(HALVES):
        mesh_grad[:, cols[n]] = upstream[:, cols[n]] + dot(near_t[1], backs[n])
    result[...] = (upd[...].astype(F32) + proc_pre * proc_sig).astype(BF16)
    result_copy = local(result, result_h.at[0], out_sem.at[CHUNKS])
    turn_x(1)
    turn_x(2)

    partial = [0.0] * HALVES
    for h in range(HALVES):
        received(2, h, push_in)
        landed = mesh_grad[:, cols[h]]
        for slot in range(2):
            landed = landed + push_in[slot, :, cols[h]].astype(F32)
        landed = (landed * mesh_slope[:, cols[h]]).astype(BF16)
        for n in range(HALVES):
            partial[n] = partial[n] + dot_t(landed, agg_w[cols[n], cols[h]])
            if h == HALVES - 1:
                agg[:, cols[n]] = partial[n].astype(BF16)
                both(lambda off: halo(3, n, agg, agg_in, off).start())

    for i in range(CHUNKS):
        span = pl.ds(i * step, step)
        own_grad[span] = dot(wide_own_t[span], agg[...])
    turn_x(3)

    def deltas(h):
        received(3, h, agg_in)
        sides = agg_in[:, :, cols[h]].reshape(2 * rows, half)
        for i in range(CHUNKS):
            span = pl.ds(i * step, step)
            grad = own_grad[span, cols[h]] + dot(wide_side_t[span], sides)
            enc_delta[span, cols[h]] = (grad * slopes[span, cols[h]]).astype(BF16)

    def grid_part(i):
        span = pl.ds(i * step, step)
        grid_out[span] = dot_t(enc_delta[span], enc_w[...]).astype(BF16)
        return local(grid_out.at[span], grid_h.at[0, span], out_sem.at[i])

    if not fused:
        for h in range(HALVES):
            deltas(h)
        for i in range(CHUNKS):
            part[i] = dot(x_t[i], enc_delta[...]) * scale
        final_copy = local(part, final_h, out_sem.at[CHUNKS + 1])
        grid_copies = [grid_part(i) for i in range(CHUNKS)]
    else:
        share = part.shape[2]
        mine = share // members

        def pair(z):
            return pltpu.make_async_remote_copy(
                src_ref=part_out.at[z, 1 - core], dst_ref=pair_in.at[z],
                send_sem=a_send.at[z], recv_sem=a_recv.at[z],
                device_id={"grid": me + 1 - 2 * core}, device_id_type=MESH)

        odd = lax.rem(ens, 2)
        first_far = (3 - 2 * odd, 2, 1 + 2 * odd) if members == 4 else tuple(range(1, members))

        def across(z, d, arriving):
            peer = lax.rem(ens + d, members)
            slot = peer if arriving else ens
            return pltpu.make_async_remote_copy(
                src_ref=quarter_out.at[z, peer], dst_ref=ens_in.at[z, slot],
                send_sem=b_send.at[z, peer], recv_sem=b_recv.at[z, slot],
                device_id={"ens": peer}, device_id_type=MESH)

        def along(d, arriving):
            peer = lax.rem(level + d, levels)
            slot = peer if arriving else level
            return pltpu.make_async_remote_copy(
                src_ref=summed_out.at[peer], dst_ref=z_in.at[slot],
                send_sem=c_send.at[peer], recv_sem=c_recv.at[slot],
                device_id={"grid": peer * 2 + core}, device_id_type=MESH)

        def gather(d, arriving):
            peer = lax.rem(ens + d, members)
            slot = peer if arriving else ens
            return pltpu.make_async_remote_copy(
                src_ref=final.at[ens], dst_ref=final.at[slot],
                send_sem=d_send.at[peer], recv_sem=d_recv.at[slot],
                device_id={"ens": peer}, device_id_type=MESH)

        order = [lax.rem(level + d, levels) for d in list(range(1, levels)) + [0]]
        def weigh(z, h):
            value = (dot(x_t[z], enc_delta[:, cols[h]]) * scale).reshape(2, share, half)
            part[z, :, :, cols[h]] = value
            part_out[z, :, :, cols[h]] = value.astype(BF16)
            if h == HALVES - 1:
                pair(z).start()

        def pair_up(z):
            pair(z).wait_recv()
            value = part[z, core] + pair_in[z].astype(F32)
            value = value.reshape(members, mine, width)
            quarter[z] = value
            quarter_out[z] = value.astype(BF16)
            for d in first_far:
                across(z, d, False).start()

        def add_up(z):
            value = quarter[z, ens]
            for d in range(1, members):
                across(z, d, True).wait_recv()
                value = value + ens_in[z, lax.rem(ens + d, members)].astype(F32)
            return value

        for h in range(HALVES - 1):
            deltas(h)
            for z in order:
                weigh(z, h)
        deltas(HALVES - 1)
        weigh(order[0], HALVES - 1)
        for n in range(1, levels):
            weigh(order[n], HALVES - 1)
            pair_up(order[n - 1])
        grid_copies = [grid_part(0)]
        pair_up(order[-1])
        grid_copies.append(grid_part(1))
        for n in range(levels - 1):
            summed_out[order[n]] = add_up(order[n]).astype(BF16)
            along(n + 1, False).start()
            if n + 2 < CHUNKS:
                grid_copies.append(grid_part(n + 2))
        summed[...] = add_up(level)
        value = summed[...]
        for d in range(1, levels):
            along(d, True).wait_recv()
            value = value + z_in[lax.rem(level + d, levels)].astype(F32)
        final[ens] = value.astype(BF16)
        for d in range(1, members):
            gather(d, False).start()
        for d in range(1, members):
            gather(d, True).wait_recv()
        final_out[...] = final[...].astype(F32)
        final_copy = local(final_out, final_h, out_sem.at[CHUNKS + 1])
        for z in order:
            pair(z).wait_send()
            for d in range(1, members):
                across(z, d, False).wait_send()
        for d in range(1, levels):
            along(d, False).wait_send()
        for d in range(1, members):
            gather(d, False).wait_send()

    for turn, landing in enumerate((panel_in, upd_in, push_in, agg_in)):
        for h in range(HALVES):
            sent(turn, h, landing)
    result_copy.wait()
    for copy in grid_copies:
        copy.wait()
    final_copy.wait()


def leave(result, grid_grad, grad, result_out, grid_out, grad_out, one, two, three, in_sem, out_sem):
    step = grid_grad.shape[1] // CHUNKS
    moves = [(result, one, result_out), (grad, three, grad_out)]
    for i in range(CHUNKS):
        span = pl.ds(i * step, step)
        moves.append((grid_grad.at[:, span], two.at[:, span], grid_out.at[:, span]))
    arriving = [pltpu.make_async_copy(a, b, in_sem.at[i]) for i, (a, b, c) in enumerate(moves)]
    leaving = [pltpu.make_async_copy(b, c, out_sem.at[i]) for i, (a, b, c) in enumerate(moves)]
    for copy in arriving:
        copy.start()
    for first, second in zip(arriving, leaving):
        first.wait()
        second.start()
    for copy in leaving:
        copy.wait()


def on_device(
    bands, members,
    grid_latent, mesh_latent, cotangent, edge_weights, edge_targets, mesh_weights, mesh_sources,
    encode_weight, aggregate_weight, process_weight,
):
    unused, total, width = grid_latent.shape
    rows = mesh_latent.shape[1]
    share = width // bands
    levels = max(bands // 2, 1)
    fused = bands % 2 == 0 and levels == CHUNKS and share % (16 * members) == 0
    scale = 1.0 / float(members * total * bands) ** 0.5
    mine = share // members if fused else 16
    gshape = (CHUNKS, 2, width // CHUNKS // 2, width) if fused else (CHUNKS, width // CHUNKS, width)
    last = (members, mine, width) if fused else gshape
    vm = pltpu.VMEM
    dma = pltpu.SemaphoreType.DMA
    panel = (2, rows, width)
    quarters = (CHUNKS, members, mine, width)
    scratch = [
        vm((total, width), BF16), vm((rows, width), BF16), vm((rows, width), BF16),
        vm(edge_weights.shape, BF16),
        pltpu.SMEM(edge_targets.shape[::-1], jnp.int32), vm(mesh_weights.shape[1:], BF16),
        pltpu.SMEM(mesh_sources.shape, jnp.int32),
        vm((width, width), BF16), vm((width, width), BF16), vm((width, width), BF16),
        vm((3 * rows, total), BF16), vm((total, rows), BF16), vm((total, 2 * rows), BF16),
        vm((3, rows, rows), BF16), vm((3, rows, rows), BF16), vm((CHUNKS, width // CHUNKS, total), BF16),
        vm((total, width), F32), vm((3 * rows, width), F32),
        vm(panel, BF16), vm(panel, BF16), vm((rows, width), BF16), vm(panel, BF16),
        vm(panel, BF16), vm(panel, BF16), vm((rows, width), BF16), vm(panel, BF16),
        vm((rows, width), F32), vm((rows, width), F32),
        vm((total, width), F32), vm((total, width), BF16), vm((total, width), BF16), vm((rows, width), BF16),
        vm(gshape, F32), vm(gshape, BF16), vm((CHUNKS, width // CHUNKS // 2, width), BF16),
        vm(quarters, F32), vm(quarters, BF16), vm(quarters, BF16),
        vm((mine, width), F32), vm((CHUNKS, mine, width), BF16), vm((CHUNKS, mine, width), BF16),
        vm((members, mine, width), BF16), vm((members, mine, width), F32),
        dma((9 + CHUNKS,)), dma((CHUNKS + 2,)), dma((4, 2, HALVES)), dma((4, 2, HALVES)),
        dma((CHUNKS,)), dma((CHUNKS,)), dma((CHUNKS, members)), dma((CHUNKS, members)),
        dma((CHUNKS,)), dma((CHUNKS,)), dma((members,)), dma((members,)),
    ]
    hbm = pl.BlockSpec(memory_space=pltpu.HBM)
    anywhere = pl.BlockSpec(memory_space=pl.ANY)
    result, grid_grad, grad = pl.pallas_call(
        functools.partial(kernel, bands, members, scale, fused),
        out_shape=(
            jax.ShapeDtypeStruct(mesh_latent.shape, BF16),
            jax.ShapeDtypeStruct(grid_latent.shape, BF16),
            jax.ShapeDtypeStruct(last, F32),
        ),
        in_specs=[hbm] * 10,
        out_specs=(anywhere,) * 3,
        scratch_shapes=scratch,
        compiler_params=pltpu.CompilerParams(
            collective_id=0, has_side_effects=True, vmem_limit_bytes=63 * 1024 * 1024
        ),
    )(
        grid_latent, mesh_latent, cotangent, edge_weights, edge_targets.T, mesh_weights, mesh_sources,
        encode_weight, aggregate_weight, process_weight,
    )
    if fused:
        result, grid_grad, grad = pl.pallas_call(
            leave,
            out_shape=tuple(jax.ShapeDtypeStruct(a.shape, a.dtype) for a in (result, grid_grad, grad)),
            in_specs=[anywhere] * 3,
            out_specs=(hbm,) * 3,
            scratch_shapes=[vm(a.shape, a.dtype) for a in (result, grid_grad, grad)] + [dma((2 + CHUNKS,))] * 2,
            compiler_params=pltpu.CompilerParams(vmem_limit_bytes=63 * 1024 * 1024),
        )(result, grid_grad, grad)
        grad = grad.reshape(share, width)
    else:
        summed = lax.psum(grad.reshape(width, width), ("ens", "grid"))
        grad = lax.dynamic_slice_in_dim(summed, lax.axis_index("grid") * share, share, 0)
    return result, grid_grad, grad


def solution(mesh):
    return jax.shard_map(
        functools.partial(on_device, mesh.shape["grid"], mesh.shape["ens"]),
        mesh=mesh,
        in_specs=(
            P("ens", "grid", None),
            P("ens", "grid", None),
            P("ens", "grid", None),
            P("grid", None, None, None),
            P("grid", None),
            P("grid", None, None, None),
            P("grid", None),
            P(),
            P(),
            P(),
        ),
        out_specs=(P("ens", "grid", None), P("ens", "grid", None), P("grid", None)),
        check_vma=False,
    )
```
